128 devices in a mesh: dp: 4 (over z), expert: 32 (over x, y, core).
Axes of the slice: x: 4, y: 4, z: 4, core: 2. Of those that a mesh axis runs over, the one named last changes fastest.
Arguments:
- tokens: bfloat16 [16384, 1024], P(('dp', 'expert')), may hold values from -6 to 6
- cotangent: bfloat16 [16384, 1024], P(('dp', 'expert')), may hold values from -6 to 6
- routes_first: int32 [16384, 1], P(('dp', 'expert')), may hold values from 0 to 31; in each aligned block of 64 rows (0 to 63, 64 to 127, ...) at most 4 rows name the same one
- routes_second: int32 [16384, 1], P(('dp', 'expert')), may hold values from 0 to 63; in each aligned block of 64 rows (0 to 63, 64 to 127, ...) at most 2 rows name the same one
- inner_first: bfloat16 [1024, 3072], P('expert'), may hold values from -0.1875 to 0.1875
- outer_first: bfloat16 [1024, 1024], P('expert'), may hold values from -0.5 to 0.5
- widen_first: bfloat16 [1024, 4096], P('expert'), may hold values from -0.1875 to 0.1875
- narrow_first: bfloat16 [4096, 1024], P('expert'), may hold values from -0.09375 to 0.09375
- mixer_first: bfloat16 [1024, 2], P('expert'), may hold values from -0.1875 to 0.1875
- gain_first: bfloat16 [1024], P('expert'), may hold values from 0.5 to 1.5
- regain_first: bfloat16 [1024], P('expert'), may hold values from 0.5 to 1.5
- inner_second: bfloat16 [1024, 3072], P('expert'), may hold values from -0.1875 to 0.1875
- outer_second: bfloat16 [1024, 1024], P('expert'), may hold values from -0.5 to 0.5
- widen_second: bfloat16 [1024, 4096], P('expert'), may hold values from -0.1875 to 0.1875
- narrow_second: bfloat16 [4096, 1024], P('expert'), may hold values from -0.09375 to 0.09375
- mixer_second: bfloat16 [1024, 2], P('expert'), may hold values from -0.1875 to 0.1875
- gain_second: bfloat16 [1024], P('expert'), may hold values from 0.5 to 1.5
- regain_second: bfloat16 [1024], P('expert'), may hold values from 0.5 to 1.5
- expand_first: bfloat16 [32, 1024, 4096], P('expert', None, 'dp'), may hold values from -0.1875 to 0.1875
- reduce_first: bfloat16 [32, 4096, 1024], P('expert', 'dp'), may hold values from -0.09375 to 0.09375
- expand_second: bfloat16 [128, 1024, 2048], P(('dp', 'expert')), may hold values from -0.1875 to 0.1875
- reduce_second: bfloat16 [128, 2048, 1024], P(('dp', 'expert')), may hold values from -0.09375 to 0.09375
Outputs:
- first_output: bfloat16 [16384, 1024], P(('dp', 'expert'))
- second_output: bfloat16 [16384, 1024], P(('dp', 'expert'))
- gradient_tokens: float32 [16384, 1024], P(('dp', 'expert'))
- gradient_inner_first: float32 [1024, 3072], P('expert')
- gradient_outer_first: float32 [1024, 1024], P('expert')
- gradient_widen_first: float32 [1024, 4096], P('expert')
- gradient_narrow_first: float32 [4096, 1024], P('expert')
- gradient_mixer_first: float32 [1024, 2], P('expert')
- gradient_gain_first: float32 [1024], P('expert')
- gradient_regain_first: float32 [1024], P('expert')
- gradient_inner_second: float32 [1024, 3072], P('expert')
- gradient_outer_second: float32 [1024, 1024], P('expert')
- gradient_widen_second: float32 [1024, 4096], P('expert')
- gradient_narrow_second: float32 [4096, 1024], P('expert')
- gradient_mixer_second: float32 [1024, 2], P('expert')
- gradient_gain_second: float32 [1024], P('expert')
- gradient_regain_second: float32 [1024], P('expert')
- gradient_expand_first: float32 [32, 1024, 4096], P('expert', None, 'dp')
- gradient_reduce_first: float32 [32, 4096, 1024], P('expert', 'dp')
- gradient_expand_second: float32 [128, 1024, 2048], P(('dp', 'expert'))
- gradient_reduce_second: float32 [128, 2048, 1024], P(('dp', 'expert'))
The draws below stay inside these ranges and needn't reach their ends.
Inputs may be any that keep to these rules, and one draw needn't show every extreme that they name: `routes_first`: in each aligned block of 64 rows (one sequence) no expert is named by more than 4 rows. `routes_second`: in each aligned block of 64 rows (one sequence) no expert is named by more than 2 rows.
All inputs are finite; a program needn't handle non-finite values.
Results may differ from the reference program's by a relative error of at most 0.035.
Values may be sent and summed in bfloat16 or wider, within the bound.
No kernel may reach another device: no remote copies, remote signals or barrier semaphores. Data moves between devices by JAX's collectives and lax.ppermute only.
A program may use at most 320 MiB of HBM per device.

```python
import math
import jax
import jax.numpy as jnp
import numpy as np
from jax import lax

D = 1024
HEADS = 16
HEAD = 64
FF = 4096
SEQ = 64
TOK_DEV = 128
TOKENS = 16384
FIRST_EXPERTS = 32
SECOND_EXPERTS = 64
FIRST_CAP = 4
SECOND_CAP = 2
FIRST_SLICE = 1024
SECOND_SLICE = 2048
N_DP = 4
N_EXPERT = 32
DEVICES = 128


def level_of(own_key, dims, cuts, smallest, largest):
    factor_of, own = 1.0, jax.random.fold_in(own_key, 6)
    for axis_at, parts in cuts:
        steps = jnp.exp(jax.random.uniform(jax.random.fold_in(own, axis_at), (parts,), jnp.float32, smallest / len(cuts), largest / len(cuts)))
        factor_of = factor_of * jnp.repeat(steps, dims[axis_at] // parts).reshape([-1 if axis == axis_at else 1 for axis in range(len(dims))])
    return factor_of


def deal_out(rng, own, number, rows, count, top, bound, lean):
    sequence = jax.random.permutation(rng, count)
    packed, common = portions_of(count, rows * top, bound, lean, True), portions_of(count, rows * top, bound, lean, False)
    places = jnp.arange(count)

    def named(sizes, turn):
        used = int((sizes > 0).sum())
        fixed = max(1, used // 4)
        moved = fixed + (places - fixed + turn * (used - fixed)) % max(1, count - fixed)
        return jnp.zeros((count,), jnp.int32).at[sequence[jnp.where(places < fixed, places, moved)]].set(jnp.asarray(sizes, jnp.int32))

    sizes = jnp.where(number % 4 == 0, named(packed, number // 4), named(common, number - number // 4 - 1))
    mixed = jax.random.permutation(jax.random.fold_in(own, 3), count)
    source_of, taker = mixed[0:count // 2 * 2:2], mixed[1:count // 2 * 2:2]
    slack = jnp.minimum(sizes[source_of] - 1, bound - sizes[taker]) // 2
    slack = jnp.where((source_of == sequence[0]) | (taker == sequence[0]) | (sizes[taker] == 0), 0, jnp.maximum(slack, 0))
    moved = jax.random.randint(jax.random.fold_in(own, 4), (count // 2,), 0, 1 << 20) % (slack + 1)
    sizes = sizes.at[source_of].add(-moved).at[taker].add(moved)
    items = jnp.searchsorted(jnp.cumsum(sizes), jnp.arange(rows * top), side="right").astype(jnp.int32)
    grid = items.reshape(top, rows).T
    grid = grid[jax.random.permutation(jax.random.fold_in(own, 1), rows)]
    turn = jax.random.randint(jax.random.fold_in(own, 2), (rows, 1), 0, top)
    return jnp.take_along_axis(grid, (jnp.arange(top)[None, :] + turn) % top, axis=1)


def portions_of(count, total, reach, lean, full):
    weights = [(1 << 20) // math.isqrt(grade ** lean) + 1 for grade in range(1, count + 1)]
    largest = reach if full else min(reach, max(-(-total // count), total * weights[0] // sum(weights)))
    least = 1 if total - largest >= count - 1 else 0
    holding, spare = [largest] + [least] * (count - 1), total - largest - least * (count - 1)
    while spare > 0:
        movable = [i for i in range(1, count) if holding[i] < largest] or [i for i in range(1, count) if holding[i] < reach]
        mass, budget = sum([weights[i] for i in movable]), spare
        for i in movable:
            extra = min(reach - holding[i], max(1, budget * weights[i] // mass), spare)
            holding[i] = holding[i] + extra
            spare = spare - extra
    return np.array(holding)


def noise(key, shape, deviation, bound, cuts=(), kind=jnp.bfloat16):
    entries = jax.random.normal(key, shape, jnp.float32) * deviation
    if len(cuts) > 0:
        entries = level_of(key, shape, cuts, -0.22, 0.18) * entries
    return jnp.clip(entries, min=-bound, max=bound).astype(kind)


def setup_inputs(seed: int = 0) -> dict:
    streams_of = jax.random.split(jax.random.key(seed), 23)
    tokens = noise(streams_of[0], (TOKENS, D), 1.0, 6.0, ((0, 128),))
    cotangent = noise(streams_of[1], (TOKENS, D), 1.0, 6.0, ((0, 128),))
    routes_first_keys = jax.random.split(jax.random.fold_in(streams_of[2], 1), TOKENS // SEQ)
    routes_first_turns = jax.random.permutation(jax.random.fold_in(streams_of[2], 3), TOKENS // SEQ)
    routes_first = jax.vmap(lambda own, number: deal_out(jax.random.fold_in(streams_of[2], 2), own, number, SEQ, FIRST_EXPERTS, 1, FIRST_CAP, 2))(routes_first_keys, routes_first_turns).reshape((TOKENS, 1))
    routes_second_keys = jax.random.split(jax.random.fold_in(streams_of[3], 1), TOKENS // SEQ)
    routes_second_turns = jax.random.permutation(jax.random.fold_in(streams_of[3], 3), TOKENS // SEQ)
    routes_second = jax.vmap(lambda own, number: deal_out(jax.random.fold_in(streams_of[3], 2), own, number, SEQ, SECOND_EXPERTS, 1, SECOND_CAP, 2))(routes_second_keys, routes_second_turns).reshape((TOKENS, 1))
    inner_first = noise(streams_of[4], (D, 3 * D), D ** -0.5, 0.1875, ((0, 32),))
    outer_first = noise(streams_of[5], (D, D), (D // 8) ** -0.5, 0.5, ((0, 32),))
    widen_first = noise(streams_of[6], (D, FF), D ** -0.5, 0.1875, ((0, 32),))
    narrow_first = noise(streams_of[7], (FF, D), FF ** -0.5, 0.09375, ((0, 32),))
    mixer_first = noise(streams_of[8], (D, 2), D ** -0.5, 0.1875, ((0, 32),))
    gain_first = jnp.clip(1.0 + 0.1 * jax.random.normal(streams_of[9], (D,), jnp.float32), 0.5, 1.5).astype(jnp.bfloat16)
    regain_first = jnp.clip(1.0 + 0.1 * jax.random.normal(streams_of[10], (D,), jnp.float32), 0.5, 1.5).astype(jnp.bfloat16)
    inner_second = noise(streams_of[11], (D, 3 * D), D ** -0.5, 0.1875, ((0, 32),))
    outer_second = noise(streams_of[12], (D, D), (D // 8) ** -0.5, 0.5, ((0, 32),))
    widen_second = noise(streams_of[13], (D, FF), D ** -0.5, 0.1875, ((0, 32),))
    narrow_second = noise(streams_of[14], (FF, D), FF ** -0.5, 0.09375, ((0, 32),))
    mixer_second = noise(streams_of[15], (D, 2), D ** -0.5, 0.1875, ((0, 32),))
    gain_second = jnp.clip(1.0 + 0.1 * jax.random.normal(streams_of[16], (D,), jnp.float32), 0.5, 1.5).astype(jnp.bfloat16)
    regain_second = jnp.clip(1.0 + 0.1 * jax.random.normal(streams_of[17], (D,), jnp.float32), 0.5, 1.5).astype(jnp.bfloat16)
    expand_first = noise(streams_of[18], (FIRST_EXPERTS, D, FF), D ** -0.5, 0.1875, ((0, 32), (2, 4)))
    reduce_first = noise(streams_of[19], (FIRST_EXPERTS, FF, D), FF ** -0.5, 0.09375, ((0, 32), (1, 4)))
    expand_second = noise(streams_of[20], (2 * SECOND_EXPERTS, D, SECOND_SLICE), D ** -0.5, 0.1875, ((0, 128),))
    reduce_second = noise(streams_of[21], (2 * SECOND_EXPERTS, SECOND_SLICE, D), FF ** -0.5, 0.09375, ((0, 128),))
    return {"tokens": tokens, "cotangent": cotangent, "routes_first": routes_first, "routes_second": routes_second, "inner_first": inner_first, "outer_first": outer_first, "widen_first": widen_first, "narrow_first": narrow_first, "mixer_first": mixer_first, "gain_first": gain_first, "regain_first": regain_first, "inner_second": inner_second, "outer_second": outer_second, "widen_second": widen_second, "narrow_second": narrow_second, "mixer_second": mixer_second, "gain_second": gain_second, "regain_second": regain_second, "expand_first": expand_first, "reduce_first": reduce_first, "expand_second": expand_second, "reduce_second": reduce_second}


@jax.custom_vjp
def low(v):
    return lax.optimization_barrier(v.astype(jnp.bfloat16)).astype(jnp.float32)

@jax.custom_vjp
def low_back(v):
    return v

def low_keep(v):
    return (low(v), None)

def low_pass(kept, grad):
    return (grad,)

def back_keep(v):
    return (v, None)

def back_low(kept, grad):
    return (low(grad),)
low.defvjp(low_keep, low_pass)
low_back.defvjp(back_keep, back_low)
highest = lax.Precision.HIGHEST
epsilon = 1e-05

def both(values):
    return low_back(low(values))

def layer_norm(values, gain):
    center = values - lax.optimization_barrier(jnp.mean(values, axis=-1, keepdims=True))
    spread = lax.optimization_barrier(jnp.mean(center * center, axis=-1, keepdims=True))
    return center * lax.rsqrt(spread + epsilon) * gain

def softmax_rows(values):
    top = lax.optimization_barrier(jnp.max(values, axis=-1, keepdims=True))
    raised = jnp.exp(values - top)
    return raised / lax.optimization_barrier(jnp.sum(raised, axis=-1, keepdims=True))

def dense_part(stream, weights):
    inner, outer, widen, narrow, mixer, gain, regain = weights
    count = stream.shape[0] // SEQ
    normed = low(layer_norm(stream, gain))
    joint = both(jnp.dot(normed, inner, precision=highest)).reshape(count, SEQ, 3, HEADS, HEAD)
    query = joint[:, :, 0]
    keys = joint[:, :, 1]
    values = joint[:, :, 2]
    scores = low_back(jnp.einsum('bqhd,bkhd->bhqk', query, keys, precision=highest) * HEAD ** (-0.5))
    causal = jnp.arange(SEQ)[:, None] >= jnp.arange(SEQ)[None, :]
    attention = softmax_rows(jnp.where(causal, scores, -1e+30))
    mixed = both(jnp.einsum('bhqk,bkhd->bqhd', low(attention), values, precision=highest)).reshape(count * SEQ, D)
    middle = stream + low_back(jnp.dot(mixed, outer, precision=highest))
    normed_two = low(layer_norm(middle, regain))
    widened = low_back(jnp.dot(normed_two, widen, precision=highest))
    active = low(jax.nn.gelu(widened))
    dense = low_back(jnp.dot(active, narrow, precision=highest))
    shares = softmax_rows(jnp.dot(normed_two, mixer, precision=highest))
    return (middle, normed_two, dense, shares)

def one_expert(rows, expander, reducer):
    total = jnp.zeros(rows.shape, jnp.float32)
    for piece in range(expander.shape[0]):
        inputs = low_back(rows)
        widened = low_back(jnp.dot(inputs, expander[piece], precision=highest))
        active = low(jax.nn.gelu(widened))
        total = total + both(jnp.dot(active, reducer[piece], precision=highest))
    return total

def expert_part(normed_two, route, expander, reducer, experts, capacity):
    sequences = normed_two.reshape(-1, SEQ, D)
    chosen = route.reshape(-1, SEQ)
    one_hot = (chosen[:, :, None] == jnp.arange(experts, dtype=jnp.int32)[None, None, :]).astype(jnp.int32)
    position = lax.optimization_barrier(jnp.sum((jnp.cumsum(one_hot, axis=1) - 1) * one_hot, axis=2))
    slot = chosen * capacity + position
    table = (slot[:, :, None] == jnp.arange(experts * capacity, dtype=jnp.int32)[None, None, :]).astype(jnp.float32)
    buffer = jnp.einsum('bsc,bsd->bcd', table, sequences, precision=highest)
    blocks = buffer.shape[0]
    grouped = buffer.reshape(blocks, experts, capacity, D).transpose(1, 0, 2, 3).reshape(experts, blocks * capacity, D)
    results = lax.map(jax.checkpoint(lambda item: one_expert(item[0], item[1], item[2])), (grouped, expander, reducer))
    back = results.reshape(experts, blocks, capacity, D).transpose(1, 0, 2, 3).reshape(blocks, experts * capacity, D)
    return jnp.einsum('bsc,bcd->bsd', table, back, precision=highest).reshape(-1, D)

def one_layer(stream, weights, route, expander, reducer, experts, capacity):
    middle, normed_two, dense, shares = lax.map(jax.checkpoint(lambda rows: dense_part(rows, weights)), stream.reshape(DEVICES, TOK_DEV, D))
    expert = expert_part(normed_two, route, expander, reducer, experts, capacity).reshape(DEVICES, TOK_DEV, D)
    return (middle + shares[..., 0:1] * dense + shares[..., 1:2] * expert).reshape(TOKENS, D)

def reference(tokens, cotangent, routes_first, routes_second, inner_first, outer_first, widen_first, narrow_first, mixer_first, gain_first, regain_first, inner_second, outer_second, widen_second, narrow_second, mixer_second, gain_second, regain_second, expand_first, reduce_first, expand_second, reduce_second):
    arrays = [tokens, inner_first, outer_first, widen_first, narrow_first, mixer_first, gain_first, regain_first, inner_second, outer_second, widen_second, narrow_second, mixer_second, gain_second, regain_second, expand_first, reduce_first, expand_second, reduce_second]
    floats = [item.astype(jnp.float32) for item in arrays]

    def forward(*inputs):
        stream = inputs[0]
        first_weights = inputs[1:8]
        second_weights = inputs[8:15]
        first_expand = inputs[15].reshape(FIRST_EXPERTS, D, N_DP, FIRST_SLICE).transpose(0, 2, 1, 3)
        first_reduce = inputs[16].reshape(FIRST_EXPERTS, N_DP, FIRST_SLICE, D)
        second_expand = inputs[17].reshape(N_DP // 2, 2, N_EXPERT, D, SECOND_SLICE).transpose(0, 2, 1, 3, 4).reshape(SECOND_EXPERTS, 2, D, SECOND_SLICE)
        second_reduce = inputs[18].reshape(N_DP // 2, 2, N_EXPERT, SECOND_SLICE, D).transpose(0, 2, 1, 3, 4).reshape(SECOND_EXPERTS, 2, SECOND_SLICE, D)
        first = one_layer(stream, first_weights, routes_first, first_expand, first_reduce, FIRST_EXPERTS, FIRST_CAP)
        second = one_layer(first, second_weights, routes_second, second_expand, second_reduce, SECOND_EXPERTS, SECOND_CAP)
        return (first, second)
    (first, second), pullback = jax.vjp(forward, *floats)
    gradients = pullback((jnp.zeros_like(first), cotangent.astype(jnp.float32)))
    return (first.astype(jnp.bfloat16), second.astype(jnp.bfloat16), gradients[0], gradients[1], gradients[2], gradients[3], gradients[4], gradients[5], gradients[6], gradients[7], gradients[8], gradients[9], gradients[10], gradients[11], gradients[12], gradients[13], gradients[14], gradients[15], gradients[16], gradients[17], gradients[18])
```

```python
import jax
import jax.numpy as jnp
from jax import lax
from jax.sharding import Mesh, PartitionSpec as P

HEADS = 16
HEAD = 64
SEQ = 64
ALL = ("z", "x", "y", "c")
PLANE = ("x", "y")
SIZES = {"z": 4, "x": 4, "y": 4, "c": 2}
highest = lax.Precision.HIGHEST
epsilon = 1e-05
bf16 = jnp.bfloat16
f32 = jnp.float32


def shift(value, axis, step):
    size = SIZES[axis]
    return lax.ppermute(value, axis, [(i, (i + step) % size) for i in range(size)])


def swap(value):
    return shift(value, "c", 1)


def dot(a, b):
    return jnp.dot(a, b, preferred_element_type=f32)


def dot_tn(a, b):
    return lax.dot_general(a, b, (((0,), (0,)), ((), ())), preferred_element_type=f32)


def dot_nt(a, b):
    return lax.dot_general(a, b, (((1,), (1,)), ((), ())), preferred_element_type=f32)


def in_order(core, mine, twin, axis):
    return jnp.where(
        core == 0,
        jnp.concatenate([mine, twin], axis=axis),
        jnp.concatenate([twin, mine], axis=axis),
    )


def half_of(value, which, axis):
    size = value.shape[axis] // 2
    return lax.dynamic_slice_in_dim(value, which * size, size, axis)


def layer_norm(values, gain):
    center = values - jnp.mean(values, axis=-1, keepdims=True)
    spread = jnp.mean(center * center, axis=-1, keepdims=True)
    return center * lax.rsqrt(spread + epsilon) * gain


def softmax_rows(values):
    top = jnp.max(values, axis=-1, keepdims=True)
    raised = jnp.exp(values - top)
    return raised / jnp.sum(raised, axis=-1, keepdims=True)


def gather_column(value):
    group = jnp.concatenate(
        [value, shift(value, "z", 1), shift(value, "z", -1), shift(value, "z", 2)], axis=0
    )
    return jnp.concatenate([group, swap(group)], axis=0)


def scatter_column(terms):
    rows = terms.shape[0] // 8
    half = terms[: 4 * rows] + swap(terms[4 * rows :].astype(bf16)).astype(f32)
    low = half[rows:].astype(bf16)
    return (
        half[:rows]
        + shift(low[:rows], "z", -1).astype(f32)
        + shift(low[rows : 2 * rows], "z", 1).astype(f32)
        + shift(low[2 * rows :], "z", 2).astype(f32)
    )


def sum_over_z(value):
    own = value.astype(f32)
    opposite = shift(value, "z", 2).astype(f32)
    before = shift(value, "z", 1).astype(f32)
    after = shift(value, "z", -1).astype(f32)
    return (own + opposite) + (before + after)


def gather_over_z(value):
    ahead = [value, shift(value, "z", -1), shift(value, "z", 2), shift(value, "z", 1)]
    twice = jnp.stack(ahead + ahead[:3])
    start = lax.rem(4 - lax.axis_index("z"), 4)
    return lax.dynamic_slice_in_dim(twice, start, 4, 0)


def positions(route):
    chosen = route[:, 0]
    row = jnp.arange(chosen.shape[0], dtype=jnp.int32)
    earlier = (row[None, :] < row[:, None]) & (row[None, :] // SEQ == row[:, None] // SEQ)
    same = (chosen[None, :] == chosen[:, None]) & earlier
    return chosen, row // SEQ, jnp.sum(same.astype(jnp.int32), axis=1)


def table_first(route):
    chosen, sequence, position = positions(route)
    slot = chosen * 8 + sequence * 4 + position
    column = jnp.arange(1024, dtype=jnp.int32) % 256
    return (slot[:, None] == column[None, :]).astype(bf16)


def table_second(route):
    chosen, sequence, position = positions(route)
    slot = (chosen // 32) * 256 + (chosen % 32) * 8 + sequence * 2 + position
    column = jnp.arange(1024, dtype=jnp.int32)
    column = (column // 512) * 256 + column % 256
    rows = (slot[:, None] == column[None, :]).astype(bf16)
    grads = ((slot + 4)[:, None] == column[None, :]).astype(bf16)
    return jnp.concatenate([rows, grads], axis=0)


def exchange(rows):
    blocks = rows.reshape(128, 8, rows.shape[-1])
    moved = lax.all_to_all(blocks, ALL, split_axis=0, concat_axis=0, tiled=True)
    return moved.reshape(rows.shape)


def gelu_slope(widened, gradient):
    return jax.vjp(jax.nn.gelu, widened)[1](gradient)[0].astype(bf16)


def pack_attention(inner, outer, mixer, gain, regain):
    blank = jnp.zeros((inner.shape[0], 124), bf16)
    return jnp.concatenate([inner, outer, mixer, gain[:, None], regain[:, None], blank], axis=1)


def unpack_attention(packed):
    return (
        packed[:, :3072],
        packed[:, 3072:4096],
        packed[:, 4096:4098],
        packed[:, 4098].astype(f32),
        packed[:, 4099].astype(f32),
    )


def pack_feed(widen, narrow):
    z, c = lax.axis_index("z"), lax.axis_index("c")
    units = widen.reshape(32, 16, 2, 4, 32)
    units = lax.dynamic_index_in_dim(units, z, 3, keepdims=False)
    mine = lax.dynamic_index_in_dim(units, c, 2, keepdims=False).reshape(32, 512)
    other = lax.dynamic_index_in_dim(units, 1 - c, 2, keepdims=False).reshape(32, 512)
    columns = in_order(c, mine, swap(other), 1)
    rows = lax.dynamic_slice_in_dim(narrow, z * 32, 32, 0)
    return jnp.concatenate([columns, rows], axis=0)


def unpack_feed(packed):
    widen = packed[:, :32].reshape(16, 32, 2, 512).transpose(0, 2, 1, 3).reshape(1024, 512)
    return widen, packed[:, 32:].reshape(512, 1024)


def attention_forward(stream, weights):
    inner, outer, mixer, gain, regain = weights
    length = stream.shape[0]
    normed = layer_norm(stream, gain).astype(bf16)
    joint = dot(normed, inner).astype(bf16).reshape(length // SEQ, SEQ, 3, HEADS, HEAD)
    query, keys, values = joint[:, :, 0], joint[:, :, 1], joint[:, :, 2]
    scores = jnp.einsum("bqhd,bkhd->bhqk", query, keys, preferred_element_type=f32) * HEAD**-0.5
    causal = jnp.arange(SEQ)[:, None] >= jnp.arange(SEQ)[None, :]
    attention = softmax_rows(jnp.where(causal, scores, -1e30))
    mixed = (
        jnp.einsum("bhqk,bkhd->bqhd", attention.astype(bf16), values, preferred_element_type=f32)
        .astype(bf16)
        .reshape(length, HEADS * HEAD)
    )
    middle = stream + dot(mixed, outer)
    normed_two = layer_norm(middle, regain).astype(bf16)
    shares = softmax_rows(dot(normed_two, mixer))
    return normed, (query, keys, values), attention, mixed, middle, normed_two, shares


def feed_forward(rows, widen, narrow):
    widened = dot(rows, widen)
    active = jax.nn.gelu(widened).astype(bf16)
    return widened, active, dot(active, narrow)


def feed_backward(rows, widen, narrow, widened, active, incoming):
    grad_widened = gelu_slope(widened, dot_nt(incoming, narrow))
    grad_rows = dot_nt(grad_widened, widen)
    return grad_rows, dot_tn(rows, grad_widened), dot_tn(active, incoming)


def attention_backward(stream, weights, saved, upstream, dense, expert, from_feed, from_experts):
    inner, outer, mixer, gain, regain = weights
    normed, (query, keys, values), attention, mixed, middle, normed_two, shares = saved
    length = stream.shape[0]
    grad_shares = jnp.concatenate(
        [
            jnp.sum(upstream * dense, axis=1, keepdims=True),
            jnp.sum(upstream * expert, axis=1, keepdims=True),
        ],
        axis=1,
    )
    grad_logits = shares * (grad_shares - jnp.sum(shares * grad_shares, axis=1, keepdims=True))
    grad_mixer = jnp.einsum("sd,sk->kd", normed_two.astype(f32), grad_logits, precision=highest)
    from_mixer = (
        grad_logits[:, 0:1] * mixer[:, 0].astype(f32) + grad_logits[:, 1:2] * mixer[:, 1].astype(f32)
    )
    grad_normed_two = from_mixer + from_feed + from_experts
    from_norm, grad_regain = jax.vjp(layer_norm, middle, regain)[1](grad_normed_two)
    grad_middle = upstream + from_norm
    grad_attended = grad_middle.astype(bf16)
    grad_mixed = dot_nt(grad_attended, outer).astype(bf16).reshape(length // SEQ, SEQ, HEADS, HEAD)
    attention_low = attention.astype(bf16)
    grad_values = jnp.einsum(
        "bhqk,bqhd->bkhd", attention_low, grad_mixed, preferred_element_type=f32
    )
    grad_attention = jnp.einsum("bqhd,bkhd->bhqk", grad_mixed, values, preferred_element_type=f32)
    grad_scores = (
        attention * (grad_attention - jnp.sum(attention * grad_attention, axis=-1, keepdims=True))
    ).astype(bf16)
    grad_query = (
        jnp.einsum("bhqk,bkhd->bqhd", grad_scores, keys, preferred_element_type=f32) * HEAD**-0.5
    )
    grad_keys = (
        jnp.einsum("bhqk,bqhd->bkhd", grad_scores, query, preferred_element_type=f32) * HEAD**-0.5
    )
    grad_joint = (
        jnp.stack([grad_query, grad_keys, grad_values], axis=2)
        .astype(bf16)
        .reshape(length, 3 * HEADS * HEAD)
    )
    grad_normed = dot_nt(grad_joint, inner)
    from_first, grad_gain = jax.vjp(layer_norm, stream, gain)[1](grad_normed)
    small = jnp.stack([grad_mixer[0], grad_mixer[1], grad_gain, grad_regain])
    return grad_middle + from_first, grad_joint, grad_attended, small


def attention_weights(both, grad_joint, grad_attended):
    c = lax.axis_index("c")
    mine = jnp.concatenate([half_of(grad_joint, c, 1), half_of(grad_attended, c, 1)], axis=1)
    other = jnp.concatenate(
        [half_of(grad_joint, 1 - c, 1), half_of(grad_attended, 1 - c, 1)], axis=1
    )
    columns = jnp.concatenate([mine, swap(other)], axis=0)
    return jnp.concatenate(
        [
            dot_tn(both[:, :1024], columns[:, :1536]).astype(bf16),
            dot_tn(both[:, 1024:], columns[:, 1536:]).astype(bf16),
        ],
        axis=1,
    )


def reduce_gradients(attention, grad_widen, grad_narrow, small):
    c = lax.axis_index("c")
    stacked = grad_narrow.astype(bf16).reshape(16, 32, 2, 512).transpose(0, 2, 1, 3)
    few = jnp.pad(small.astype(bf16).T, ((0, 0), (0, 124)))
    packed = jnp.concatenate(
        [attention, grad_widen.astype(bf16), stacked.reshape(1024, 512), few], axis=1
    )
    summed = lax.psum_scatter(packed, PLANE, scatter_dimension=0, tiled=True)
    columns = summed.shape[1]
    rows = jnp.concatenate([summed[:, :2560], summed[:, 3072:]], axis=1)
    mine, got = half_of(rows, c, 0), swap(half_of(rows, 1 - c, 0))
    few = (mine[:, 2560:].astype(f32) + got[:, 2560:].astype(f32)).astype(bf16)
    inner = in_order(c, mine[:, :1536], got[:, :1536], 1)
    outer = in_order(c, mine[:, 1536:2048], got[:, 1536:2048], 1)
    total = sum_over_z(jnp.concatenate([inner, outer, few], axis=1))
    widen = in_order(c, mine[:, 2048:2560], got[:, 2048:2560], 1)
    narrow = summed[:, 2560:3072]
    narrow = jnp.concatenate([narrow[:32], narrow[32:]], axis=1)
    parts = gather_over_z(jnp.concatenate([widen, narrow], axis=0)).astype(f32)
    widen = parts[:, :32].reshape(4, 32, 2, 16, 32).transpose(1, 3, 2, 0, 4).reshape(32, 4096)
    narrow = parts[:, 32:].reshape(128, 1024)
    few = total[:, 4096:]
    return (
        total[:, :3072],
        total[:, 3072:4096],
        widen,
        narrow,
        few[:, 0:2],
        few[:, 2],
        few[:, 3],
    )


def on_device(
    tokens,
    cotangent,
    routes_first,
    routes_second,
    inner_first,
    outer_first,
    widen_first,
    narrow_first,
    mixer_first,
    gain_first,
    regain_first,
    inner_second,
    outer_second,
    widen_second,
    narrow_second,
    mixer_second,
    gain_second,
    regain_second,
    expand_first,
    reduce_first,
    expand_second,
    reduce_second,
):
    everyone = ("x", "y", "c")
    packed_first = pack_attention(inner_first, outer_first, mixer_first, gain_first, regain_first)
    packed_second = pack_attention(
        inner_second, outer_second, mixer_second, gain_second, regain_second
    )
    gathered_first = lax.all_gather(packed_first, everyone, axis=0, tiled=True)
    packed_feed = jnp.concatenate(
        [pack_feed(widen_first, narrow_first), pack_feed(widen_second, narrow_second)], axis=0
    )
    packed_feed, gathered_first = lax.optimization_barrier((packed_feed, gathered_first))
    gathered_feed = lax.all_gather(packed_feed, PLANE, axis=0)
    packed_second, gathered_feed = lax.optimization_barrier((packed_second, gathered_feed))
    gathered_second = lax.all_gather(packed_second, everyone, axis=0, tiled=True)
    weights_first = unpack_attention(gathered_first)
    weights_second = unpack_attention(gathered_second)
    widen_one, narrow_one = unpack_feed(gathered_feed[:, :64])
    widen_two, narrow_two = unpack_feed(gathered_feed[:, 64:])
    first_table = table_first(routes_first)
    second_table = table_second(routes_second)
    expander, reducer = expand_first[0], reduce_first[0]
    expander_two, reducer_two = expand_second[0], reduce_second[0]

    stream = tokens.astype(f32)
    saved = attention_forward(stream, weights_first)
    normed, _, _, mixed, middle, normed_two, shares = saved
    received = exchange(dot_tn(first_table, normed_two).astype(bf16))
    column = gather_column(normed_two)
    dense_widened, dense_active, dense_terms = feed_forward(column, widen_one, narrow_one)
    dense = scatter_column(dense_terms)
    widened, active, parts = feed_forward(received, expander, reducer)
    expert = dot(first_table, exchange(parts.astype(bf16)))
    own = jnp.concatenate([normed, mixed], axis=1)
    both_first = jnp.concatenate([own, swap(own)], axis=0)
    output = middle + shares[:, 0:1] * dense + shares[:, 1:2] * expert

    upstream = cotangent.astype(f32)
    saved_two = attention_forward(output, weights_second)
    normed, _, _, mixed, middle_two, normed_two, shares_two = saved_two
    grad_dense = (upstream * shares_two[:, 0:1]).astype(bf16)
    grad_expert = (upstream * shares_two[:, 1:2]).astype(bf16)
    arrived = exchange(
        dot_tn(second_table, jnp.concatenate([normed_two, grad_expert], axis=0)).astype(bf16)
    ).reshape(128, 2, 4, 1024)
    column_two = gather_column(jnp.concatenate([normed_two, grad_dense], axis=1))
    rows_two, incoming_two = column_two[:, :1024], column_two[:, 1024:]
    hidden, hidden_active, dense_terms = feed_forward(rows_two, widen_two, narrow_two)
    feed_terms, grad_widen_two, grad_narrow_two = feed_backward(
        rows_two, widen_two, narrow_two, hidden, hidden_active, incoming_two
    )
    summed = scatter_column(jnp.concatenate([dense_terms, feed_terms], axis=1))
    dense_two, from_feed = summed[:, :1024], summed[:, 1024:]
    rows = arrived[:, 0].reshape(512, 1024)
    incoming = arrived[:, 1].reshape(512, 1024)
    hidden, hidden_active, parts = feed_forward(rows, expander_two, reducer_two)
    grad_rows, grad_expand_two, grad_reduce_two = feed_backward(
        rows, expander_two, reducer_two, hidden, hidden_active, incoming
    )
    back = jnp.stack(
        [parts.astype(bf16).reshape(128, 4, 1024), grad_rows.astype(bf16).reshape(128, 4, 1024)],
        axis=1,
    )
    taken = dot(second_table, exchange(back.reshape(1024, 1024)))
    expert_two, from_experts = taken[:128], taken[128:]
    own = jnp.concatenate([normed, mixed], axis=1)
    both_second = jnp.concatenate([own, swap(own)], axis=0)
    output_two = middle_two + shares_two[:, 0:1] * dense_two + shares_two[:, 1:2] * expert_two
    upstream, grad_joint, grad_attended, small = attention_backward(
        output, weights_second, saved_two, upstream, dense_two, expert_two, from_feed, from_experts
    )

    grad_dense = (upstream * shares[:, 0:1]).astype(bf16)
    grad_expert = (upstream * shares[:, 1:2]).astype(bf16)
    incoming = exchange(dot_tn(first_table, grad_expert).astype(bf16))
    feed_incoming = gather_column(grad_dense)
    second_attention = attention_weights(both_second, grad_joint, grad_attended)
    finals_second = reduce_gradients(second_attention, grad_widen_two, grad_narrow_two, small)
    feed_terms, grad_widen_one, grad_narrow_one = feed_backward(
        column, widen_one, narrow_one, dense_widened, dense_active, feed_incoming
    )
    from_feed = scatter_column(feed_terms)
    grad_rows, grad_expand_one, grad_reduce_one = feed_backward(
        received, expander, reducer, widened, active, incoming
    )
    from_experts = dot(first_table, exchange(grad_rows.astype(bf16)))
    gradient_tokens, grad_joint, grad_attended, small = attention_backward(
        stream, weights_first, saved, upstream, dense, expert, from_feed, from_experts
    )
    first_attention = attention_weights(both_first, grad_joint, grad_attended)
    finals_first = reduce_gradients(first_attention, grad_widen_one, grad_narrow_one, small)
    return (
        (output.astype(bf16), output_two.astype(bf16), gradient_tokens)
        + finals_first
        + finals_second
        + (
            grad_expand_one[None],
            grad_reduce_one[None],
            grad_expand_two[None],
            grad_reduce_two[None],
        )
    )


def solution(mesh):
    fine = Mesh(mesh.devices.reshape(4, 4, 4, 2), ALL)
    owner = ("x", "y", "c")
    tokens = P(ALL, None)
    dense = (P(owner, None),) * 5 + (P(owner),) * 2
    experts = (
        P(owner, None, "z"),
        P(owner, "z", None),
        P(ALL, None, None),
        P(ALL, None, None),
    )
    return jax.shard_map(
        on_device,
        mesh=fine,
        in_specs=(tokens,) * 4 + dense + dense + experts,
        out_specs=(tokens,) * 3 + dense + dense + experts,
        check_vma=False,
    )
```

```python
import jax
import jax.numpy as jnp
from jax import lax
from jax.experimental import pallas as pl
from jax.experimental.pallas import tpu as pltpu
from jax.sharding import Mesh, PartitionSpec as P

HEADS = 16
HEAD = 64
SEQ = 64
ROWS = 128
D = 1024
PACKED = 4224
SCALE = HEAD**-0.5
ALL = ("z", "x", "y", "c")
PLANE = ("x", "y")
COLUMN = ("z", "c")
SIZES = {"z": 4, "x": 4, "y": 4, "c": 2}
epsilon = 1e-05
bf16 = jnp.bfloat16
f32 = jnp.float32
LIMIT = 56 * 1024 * 1024


def shift(value, axis, step):
    size = SIZES[axis]
    return lax.ppermute(value, axis, [(i, (i + step) % size) for i in range(size)])


def swap(value):
    return shift(value, "c", 1)


def flip(value):
    return lax.ppermute(value, "z", [(0, 1), (1, 0), (2, 3), (3, 2)])


def dot(a, b):
    return jnp.dot(a, b, preferred_element_type=f32)


def dot_tn(a, b):
    return lax.dot_general(a, b, (((0,), (0,)), ((), ())), preferred_element_type=f32)


def dot_nt(a, b):
    return lax.dot_general(a, b, (((1,), (1,)), ((), ())), preferred_element_type=f32)


def in_order(core, mine, twin, axis):
    return jnp.where(
        core == 0,
        jnp.concatenate([mine, twin], axis=axis),
        jnp.concatenate([twin, mine], axis=axis),
    )


def half_of(value, which, axis):
    size = value.shape[axis] // 2
    return lax.dynamic_slice_in_dim(value, which * size, size, axis)


def shape(*dims, dtype=bf16):
    return jax.ShapeDtypeStruct(dims, dtype)


def whole():
    return pl.BlockSpec(memory_space=pltpu.VMEM)


def space_of(value):
    if value.dtype == jnp.int32 and value.ndim == 1:
        return pl.BlockSpec(memory_space=pltpu.SMEM)
    return whole()


def call(body, outs, args, flops, moved, far=(), scratch=(), name=None):
    return pl.pallas_call(
        body,
        out_shape=outs,
        in_specs=[
            pl.BlockSpec(memory_space=pl.ANY) if i in far else space_of(arg)
            for i, arg in enumerate(args)
        ],
        out_specs=[whole()] * len(outs),
        scratch_shapes=list(scratch),
        compiler_params=pltpu.CompilerParams(vmem_limit_bytes=LIMIT),
        cost_estimate=pl.CostEstimate(flops=flops, bytes_accessed=moved, transcendentals=0),
        name=name,
    )(*args)


def start_weights(far, near, sems, base):
    copies = []
    for i, low, high in ((4, 4096, 4224), (0, 0, D), (1, D, 2 * D), (2, 2 * D, 3 * D), (3, 3 * D, 4096)):
        copy = pltpu.make_async_copy(
            far.at[:, base + low : base + high], near.at[:, low:high], sems.at[i]
        )
        copy.start()
        copies.append(copy)
    return copies


WEIGHTS = (pltpu.VMEM((D, PACKED), bf16), pltpu.SemaphoreType.DMA((5,)))


def vector_rows(near):
    pick = lax.broadcasted_iota(jnp.int32, (8, 128), 0) == lax.broadcasted_iota(
        jnp.int32, (8, 128), 1
    )
    return dot_nt(pick.astype(bf16), near[:, 4096:4224])


def normalize(values):
    center = values - jnp.mean(values, axis=-1, keepdims=True)
    spread = jnp.mean(center * center, axis=-1, keepdims=True)
    inverse = lax.rsqrt(spread + epsilon)
    return center * inverse, inverse


def normalize_backward(hat, inverse, gradient):
    return inverse * (
        gradient
        - jnp.mean(gradient, axis=-1, keepdims=True)
        - hat * jnp.mean(gradient * hat, axis=-1, keepdims=True)
    )


def lane_half(rows=ROWS):
    return lax.broadcasted_iota(jnp.int32, (rows, 128), 1) < HEAD


def split_heads(pair):
    first = lane_half()
    blank = jnp.zeros_like(pair)
    return jnp.concatenate([jnp.where(first, pair, blank), jnp.where(first, blank, pair)], axis=0)


def own_sequence(table):
    first = lane_half(SEQ)
    return [
        jnp.where(first, table[low : low + SEQ], table[low + SEQ : low + 2 * SEQ])
        for low in (0, ROWS)
    ]


def spread_sequences(blocks):
    first = lane_half(SEQ)
    parts = []
    for block in blocks:
        parts += [jnp.where(first, block, 0.0), jnp.where(first, 0.0, block)]
    return jnp.concatenate(parts, axis=0).astype(bf16)


def attention_of(query, keys):
    key = lax.broadcasted_iota(jnp.int32, (SEQ, ROWS), 0)
    place = jnp.bitwise_and(lax.broadcasted_iota(jnp.int32, (SEQ, ROWS), 1), SEQ - 1)
    result = []
    for scores in own_sequence(dot_nt(split_heads(keys), query) * SCALE):
        scores = jnp.where(key <= place, scores, -1e30)
        raised = jnp.exp(scores - jnp.max(scores, axis=0, keepdims=True))
        result.append(raised / jnp.sum(raised, axis=0, keepdims=True))
    return result


def pair_of(ref, part, pair):
    return ref[:, pl.ds(pl.multiple_of(part * D + pair * 128, 128), 128)]


def front(stream, near, copies, normed_out, joint_out, mixed_out, middle_out, two_out, share_out):
    copies[0].wait()
    vectors = vector_rows(near)
    hat, _ = normalize(stream)
    normed = (hat * vectors[2:3]).astype(bf16)
    normed_out[...] = normed
    for part in range(3):
        copies[part + 1].wait()
        for low in range(part * D, part * D + D, 512):
            joint_out[:, low : low + 512] = dot(normed, near[:, low : low + 512]).astype(bf16)

    @pl.loop(0, HEADS // 2, unroll=True)
    def _(pair):
        query, keys, values = (pair_of(joint_out, part, pair) for part in range(3))
        table = spread_sequences(attention_of(query, keys))
        one = dot_tn(table[0:ROWS], values)
        two = dot_tn(table[ROWS : 2 * ROWS], values)
        column = pl.ds(pl.multiple_of(pair * 128, 128), 128)
        mixed_out[:, column] = jnp.where(lane_half(), one, two).astype(bf16)

    mixed = mixed_out[...]
    copies[4].wait()
    for low in range(0, D, 512):
        middle_out[:, low : low + 512] = stream[:, low : low + 512] + dot(
            mixed, near[:, 3072 + low : 3072 + low + 512]
        )
    hat, _ = normalize(middle_out[...])
    normed_two = (hat * vectors[3:4]).astype(bf16)
    two_out[...] = normed_two
    logits = dot(normed_two, near[:, 4096:4224])
    one, two = logits[:, 0:1], logits[:, 1:2]
    top = jnp.maximum(one, two)
    one, two = jnp.exp(one - top), jnp.exp(two - top)
    total = one + two
    one, two = one / total, two / total
    lane = lax.broadcasted_iota(jnp.int32, (ROWS, 128), 1)
    share_out[...] = jnp.where(lane == 0, one, two)
    return normed_two, one, two


def send_first(rows, slot_row, out):
    slots = lax.broadcasted_iota(jnp.int32, (256, ROWS), 0)
    table = (slots == slot_row[...]).astype(bf16)
    buffer = dot(table, rows).astype(bf16)
    for z in range(4):
        out[z * 256 : (z + 1) * 256, :] = buffer


def send_second(rows, grads, slot_row, out):
    slots = lax.broadcasted_iota(jnp.int32, (256, ROWS), 0)
    for group in range(2):
        wanted = slot_row[...] - group * 256
        buffer = dot((slots == wanted).astype(bf16), rows) + dot(
            (slots == wanted + 4).astype(bf16), grads
        )
        buffer = buffer.astype(bf16)
        for z in (2 * group, 2 * group + 1):
            out[z * 256 : (z + 1) * 256, :] = buffer


def take_first(back, slot_column):
    column = lax.broadcasted_iota(jnp.int32, (ROWS, 1024), 1)
    table = (slot_column[...] == jnp.bitwise_and(column, 255)).astype(bf16)
    return dot(table, back[...])


def take_second(back, slot_column):
    column = lax.broadcasted_iota(jnp.int32, (ROWS, 1024), 1)
    place = jnp.where(column >= 512, 256, 0) + jnp.bitwise_and(column, 255)
    rows = dot((slot_column[...] == place).astype(bf16), back[...])
    grads = dot((slot_column[...] + 4 == place).astype(bf16), back[...])
    return rows, grads


def backward(
    stream,
    near,
    copies,
    joint_ref,
    middle,
    normed_two,
    one,
    two,
    upstream,
    dense,
    expert,
    incoming,
    joint_out,
    attended_out,
    small_out,
    mixed_ref,
):
    copies[0].wait()
    vectors = vector_rows(near)
    first = jnp.sum(upstream * dense, axis=1, keepdims=True)
    second = jnp.sum(upstream * expert, axis=1, keepdims=True)
    both = one * first + two * second
    first, second = one * (first - both), two * (second - both)
    normed_two = normed_two.astype(f32)
    gradient = first * vectors[0:1] + second * vectors[1:2] + incoming
    hat, inverse = normalize(middle)
    small_out[0:1, :] = jnp.sum(normed_two * first, axis=0, keepdims=True)
    small_out[1:2, :] = jnp.sum(normed_two * second, axis=0, keepdims=True)
    small_out[3:4, :] = jnp.sum(gradient * hat, axis=0, keepdims=True)
    small_out[4:8, :] = jnp.zeros((4, D), f32)
    grad_middle = upstream + normalize_backward(hat, inverse, gradient * vectors[3:4])
    attended = grad_middle.astype(bf16)
    attended_out[...] = attended
    copies[4].wait()
    for low in range(0, D, 512):
        mixed_ref[:, low : low + 512] = dot_nt(attended, near[low : low + 512, 3072:4096]).astype(
            bf16
        )

    @pl.loop(0, HEADS // 2, unroll=True)
    def _(pair):
        query, keys, values = (pair_of(joint_ref, part, pair) for part in range(3))
        column = pl.ds(pl.multiple_of(pair * 128, 128), 128)
        grad_mixed = mixed_ref[:, column]
        attention = attention_of(query, keys)
        grad_attention = own_sequence(dot_nt(split_heads(values), grad_mixed))
        grad_scores = [
            weight * (grad - jnp.sum(weight * grad, axis=0, keepdims=True))
            for weight, grad in zip(attention, grad_attention)
        ]
        grad_scores = spread_sequences(grad_scores)
        grad_keys = dot(grad_scores, query) * SCALE
        grad_values = dot(spread_sequences(attention), grad_mixed)
        halves = (
            (
                dot_tn(grad_scores[0:ROWS], keys) * SCALE,
                dot_tn(grad_scores[ROWS : 2 * ROWS], keys) * SCALE,
            ),
            (grad_keys[0:ROWS], grad_keys[ROWS : 2 * ROWS]),
            (grad_values[0:ROWS], grad_values[ROWS : 2 * ROWS]),
        )
        for part in range(3):
            place = pl.ds(pl.multiple_of(part * D + pair * 128, 128), 128)
            joint_out[:, place] = jnp.where(lane_half(), *halves[part]).astype(bf16)

    for copy in copies[1:4]:
        copy.wait()
    parts = []
    for low in range(0, D, 256):
        parts.append(dot_nt(joint_out[...], near[low : low + 256, 0:3072]))
    grad_normed = jnp.concatenate(parts, axis=1)
    hat, inverse = normalize(stream)
    small_out[2:3, :] = jnp.sum(grad_normed * hat, axis=0, keepdims=True)
    return grad_middle + normalize_backward(hat, inverse, grad_normed * vectors[2:3])


def halves_of(pair):
    return pair.at[:, 0:D], pair.at[:, D : 2 * D]


def first_front(tokens, weights, slot_row):
    def body(tokens, far, slot_row, pair, joint, middle, two, shares, send, near, sems):
        copies = start_weights(far, near, sems, 0)
        normed, mixed = halves_of(pair)
        rows, _, _ = front(
            tokens[...].astype(f32), near, copies, normed, joint, mixed, middle, two, shares
        )
        send_first(rows, slot_row, send)

    outs = (
        shape(ROWS, 2 * D),
        shape(ROWS, 3 * D),
        shape(ROWS, D, dtype=f32),
        shape(ROWS, D),
        shape(ROWS, 128, dtype=f32),
        shape(1024, D),
    )
    args = (tokens, weights, slot_row)
    return call(body, outs, args, 1300000000, 14000000, far=(1,), scratch=WEIGHTS, name="front")


def second_front(back, slot_column, middle, shares, own, parts, cotangent, weights, slot_row):
    def body(
        back,
        slot_column,
        middle,
        shares,
        own,
        part_a,
        part_b,
        part_c,
        cotangent,
        far,
        slot_row,
        low_out,
        stream_out,
        dense_out,
        expert_out,
        pair,
        joint,
        middle_out,
        feed,
        shares_out,
        send,
        near,
        sems,
    ):
        copies = start_weights(far, near, sems, PACKED)
        expert = take_first(back, slot_column)
        dense = own[...] + part_a[...].astype(f32) + part_b[...].astype(f32) + part_c[...].astype(f32)
        dense_out[...] = dense
        expert_out[...] = expert
        stream = middle[...] + shares[:, 0:1] * dense + shares[:, 1:2] * expert
        stream_out[...] = stream
        low_out[...] = stream.astype(bf16)
        normed, mixed = halves_of(pair)
        two, grad_dense = halves_of(feed)
        rows, one, other = front(
            stream, near, copies, normed, joint, mixed, middle_out, two, shares_out
        )
        upstream = cotangent[...].astype(f32)
        grad_dense[...] = (upstream * one).astype(bf16)
        send_second(rows, (upstream * other).astype(bf16), slot_row, send)

    outs = (
        shape(ROWS, D),
        shape(ROWS, D, dtype=f32),
        shape(ROWS, D, dtype=f32),
        shape(ROWS, D, dtype=f32),
        shape(ROWS, 2 * D),
        shape(ROWS, 3 * D),
        shape(ROWS, D, dtype=f32),
        shape(ROWS, 2 * D),
        shape(ROWS, 128, dtype=f32),
        shape(1024, D),
    )
    args = (back, slot_column, middle, shares, own, *parts, cotangent, weights, slot_row)
    return call(body, outs, args, 1800000000, 20000000, far=(9,), scratch=WEIGHTS, name="between")


BACK = WEIGHTS + (
    pltpu.VMEM((ROWS, D), bf16),
    pltpu.VMEM((ROWS, 3 * D), bf16),
    pltpu.VMEM((ROWS, D), bf16),
)


def second_back(
    place,
    back,
    slot_column,
    cotangent,
    middle,
    shares,
    own,
    got,
    flipped,
    feed,
    joint,
    stream,
    weights,
    first_shares,
    slot_row,
):
    def body(
        place,
        back,
        slot_column,
        cotangent,
        middle,
        shares,
        own,
        got,
        flipped,
        feed,
        joint,
        stream,
        far,
        first_shares,
        slot_row,
        low_out,
        grad_out,
        mine,
        other,
        small_out,
        grad_dense,
        send,
        near,
        sems,
        mixed,
        joint_grad,
        attended,
    ):
        copies = start_weights(far, near, sems, PACKED)
        expert, from_experts = take_second(back, slot_column)
        total = own[0:ROWS, :] + got[0:ROWS, :].astype(f32) + flipped[...].astype(f32)
        dense, from_feed = total[:, 0:D], total[:, D : 2 * D]
        one, two = shares[:, 0:1], shares[:, 1:2]
        low_out[...] = (middle[...] + one * dense + two * expert).astype(bf16)
        gradient = backward(
            stream[...],
            near,
            copies,
            joint,
            middle[...],
            feed[:, 0:D],
            one,
            two,
            cotangent[...].astype(f32),
            dense,
            expert,
            from_feed + from_experts,
            joint_grad,
            attended,
            small_out,
            mixed,
        )
        grad_out[...] = gradient
        grad_dense[...] = (gradient * first_shares[:, 0:1]).astype(bf16)
        send_first((gradient * first_shares[:, 1:2]).astype(bf16), slot_row, send)
        for out, core in ((mine, place[1]), (other, 1 - place[1])):
            wide = pl.multiple_of(core * 1536, 128)
            out[:, 0:1536] = joint_grad[:, pl.ds(wide, 1536)]
            out[:, 1536:2048] = attended[:, pl.ds(pl.multiple_of(core * 512, 128), 512)]

    outs = (
        shape(ROWS, D),
        shape(ROWS, D, dtype=f32),
        shape(ROWS, 2048),
        shape(ROWS, 2048),
        shape(8, D, dtype=f32),
        shape(ROWS, D),
        shape(1024, D),
    )
    args = (
        place,
        back,
        slot_column,
        cotangent,
        middle,
        shares,
        own,
        got,
        flipped,
        feed,
        joint,
        stream,
        weights,
        first_shares,
        slot_row,
    )
    return call(body, outs, args, 2200000000, 22000000, far=(12,), scratch=BACK, name="turn")


def first_back(
    place, back, slot_column, upstream, middle, shares, dense, expert, own, parts, normed_two, joint, tokens, weights
):
    def body(
        place,
        back,
        slot_column,
        upstream,
        middle,
        shares,
        dense,
        expert,
        own,
        part_a,
        part_b,
        part_c,
        normed_two,
        joint,
        tokens,
        far,
        grad_out,
        mine,
        other,
        small_out,
        near,
        sems,
        mixed,
        joint_grad,
        attended,
    ):
        copies = start_weights(far, near, sems, 0)
        incoming = take_first(back, slot_column)
        incoming = (
            own[...]
            + part_a[...].astype(f32)
            + part_b[...].astype(f32)
            + part_c[...].astype(f32)
            + incoming
        )
        grad_out[...] = backward(
            tokens[...].astype(f32),
            near,
            copies,
            joint,
            middle[...],
            normed_two[...],
            shares[:, 0:1],
            shares[:, 1:2],
            upstream[...],
            dense[...],
            expert[...],
            incoming,
            joint_grad,
            attended,
            small_out,
            mixed,
        )
        for out, core in ((mine, place[1]), (other, 1 - place[1])):
            for i, step in enumerate((0, 1, 3, 2)):
                index = lax.rem(place[0] + step, 4) * 2 + core
                wide = pl.ds(pl.multiple_of(index * 384, 128), 384)
                out[i, :, 0:384] = joint_grad[:, wide]
                out[i, :, 384:512] = attended[:, pl.ds(pl.multiple_of(index * 128, 128), 128)]

    outs = (
        shape(ROWS, D, dtype=f32),
        shape(4, ROWS, 512),
        shape(4, ROWS, 512),
        shape(8, D, dtype=f32),
    )
    args = (
        place,
        back,
        slot_column,
        upstream,
        middle,
        shares,
        dense,
        expert,
        own,
        *parts,
        normed_two,
        joint,
        tokens,
        weights,
    )
    return call(body, outs, args, 2000000000, 20000000, far=(15,), scratch=BACK, name="back")


def few_columns(small):
    pick = lax.broadcasted_iota(jnp.int32, (8, 128), 0) == lax.broadcasted_iota(
        jnp.int32, (8, 128), 1
    )
    return dot_tn(small[...].astype(bf16), pick.astype(bf16)).astype(bf16)


def weights_first(place, line, mine, got, parts, small):
    def body(place, line, mine, got, part_a, part_b, part_c, small, out, ordered):
        def put(step, core, value):
            index = lax.rem(place[0] + step, 4) * 2 + core
            ordered[pl.ds(pl.multiple_of(index * ROWS, ROWS), ROWS), :] = value

        own, other = place[1], 1 - place[1]
        put(0, own, mine[0])
        put(0, other, got[0])
        for step, part in ((3, part_a), (1, part_b), (2, part_c)):
            put(step, own, part[0:ROWS, :])
            put(step, other, part[ROWS : 2 * ROWS, :])
        for low in range(0, D, 256):
            rows = slice(low, low + 256)
            for left, first, last in ((low, 0, 384), (D + low, 384, 512)):
                out[rows, first:last] = dot_tn(
                    line[:, left : left + 256], ordered[:, first:last]
                ).astype(bf16)
        out[:, 512:640] = few_columns(small)

    args = (place, line, mine, got, *parts, small)
    return call(
        body,
        (shape(D, 640),),
        args,
        1100000000,
        7000000,
        scratch=(pltpu.VMEM((1024, 512), bf16),),
        name="first_weights",
    )[0]


def weights_second(packed, pair, pair_twin, mine, got, small):
    def body(packed, pair, pair_twin, mine, got, small, out, near, sem):
        for low in range(0, D, 256):
            rows = slice(low, low + 256)
            for left, first, last in ((low, 0, 1536), (D + low, 1536, 2048)):
                near[rows, first:last] = (
                    dot_tn(pair[:, left : left + 256], mine[:, first:last])
                    + dot_tn(pair_twin[:, left : left + 256], got[:, first:last])
                ).astype(bf16)
        near[:, 2048:2176] = few_columns(small)
        copy = pltpu.make_async_copy(near, out.at[:, 2048:4224], sem)
        copy.start()
        copy.wait()

    args = (packed, pair, pair_twin, mine, got, small)
    return pl.pallas_call(
        body,
        out_shape=shape(D, 4224),
        in_specs=[pl.BlockSpec(memory_space=pl.ANY)] + [whole()] * 5,
        out_specs=pl.BlockSpec(memory_space=pl.ANY),
        scratch_shapes=[pltpu.VMEM((D, 2176), bf16), pltpu.SemaphoreType.DMA(())],
        input_output_aliases={0: 0},
        compiler_params=pltpu.CompilerParams(vmem_limit_bytes=LIMIT),
        cost_estimate=pl.CostEstimate(flops=1000000, bytes_accessed=1000000, transcendentals=0),
        name="second_weights",
    )(*args)


def weights_feed(group, group_twin, grad_hidden, active, inc, inc_twin):
    def body(group, group_twin, grad_hidden, active, inc, inc_twin, out):
        for low in range(0, D, 256):
            rows = slice(low, low + 256)
            out[rows, 0:512] = (
                dot_tn(group[:, rows], grad_hidden[0:512, :])
                + dot_tn(group_twin[:, rows], grad_hidden[512:1024, :])
            ).astype(bf16)
        for low in range(0, 512, 256):
            units = slice(low, low + 256)
            narrow = (
                dot_tn(active[0:512, units], inc[...]) + dot_tn(active[512:1024, units], inc_twin[...])
            ).astype(bf16)
            for i in range(8):
                place = low * 2 + i * 64
                part = narrow[i * 32 : (i + 1) * 32, :]
                out[place : place + 32, 512:1024] = part[:, 0:512]
                out[place + 32 : place + 64, 512:1024] = part[:, 512:1024]

    args = (group, group_twin, grad_hidden, active, inc, inc_twin)
    return call(body, (shape(D, 1024),), args, 1000000, 1000000, name="feed_weights")[0]


def feed_forward(group, twin, packed):
    def body(group, twin, far, other, own, active_out, slope_out, widen, narrow, near, sem):
        copy = pltpu.make_async_copy(far, near, sem)
        copy.start()
        copy.wait()
        for i in range(16):
            rows = near[i * 64 : i * 64 + 32, :]
            widen[i * 64 : i * 64 + 32, :] = rows[:, 0:512]
            widen[i * 64 + 32 : i * 64 + 64, :] = rows[:, 512:1024]
            narrow[i * 32 : i * 32 + 32, :] = near[i * 64 + 32 : i * 64 + 64, :]
        for i, source in ((1, twin), (0, group)):
            for low in range(0, 512, 256):
                active, slope = gelu_pieces(dot(source[low : low + 256, :], widen[...]))
                active = active.astype(bf16)
                place = slice(i * 512 + low, i * 512 + low + 256)
                active_out[place, :] = active
                slope_out[place, :] = slope.astype(bf16)
                terms = dot(active, narrow[...])
                if i == 1:
                    other[low : low + 256, :] = terms.astype(bf16)
                else:
                    own[low : low + 256, :] = terms

    outs = (
        shape(512, D),
        shape(512, D, dtype=f32),
        shape(1024, 512),
        shape(1024, 512),
        shape(D, 512),
        shape(512, D),
    )
    scratch = (pltpu.VMEM((D, D), bf16), pltpu.SemaphoreType.DMA(()))
    args = (group, twin, packed)
    return call(body, outs, args, 1000000, 1000000, far=(2,), scratch=scratch, name="feed_one")


def feed_backward(group, twin, slope, widen, narrow):
    def body(group, twin, slope, widen, narrow, other, own, grad_out):
        for i, source in ((1, twin), (0, group)):
            for low in range(0, 512, 256):
                place = slice(i * 512 + low, i * 512 + low + 256)
                grad = dot_nt(source[low : low + 256, :], narrow[...]) * slope[place, :].astype(f32)
                grad = grad.astype(bf16)
                grad_out[place, :] = grad
                terms = dot_nt(grad, widen[...])
                if i == 1:
                    other[low : low + 256, :] = terms.astype(bf16)
                else:
                    own[low : low + 256, :] = terms

    outs = (shape(512, D), shape(512, D, dtype=f32), shape(1024, 512))
    args = (group, twin, slope, widen, narrow)
    return call(body, outs, args, 1000000, 1000000, name="feed_one_back")


def gelu_pieces(x):
    k = 0.7978845608028654
    square = x * x
    bend = jnp.tanh(k * (x + 0.044715 * (square * x)))
    half = 0.5 * (1.0 + bend)
    slope = half + x * (0.5 * (1.0 - bend * bend)) * (k * (1.0 + 3 * 0.044715 * square))
    return x * half, slope


def grid_call(body, grid, in_specs, outs, out_specs, scratch, args, flops, moved, name):
    return pl.pallas_call(
        body,
        grid=grid,
        in_specs=in_specs,
        out_shape=outs,
        out_specs=out_specs,
        scratch_shapes=scratch,
        compiler_params=pltpu.CompilerParams(
            vmem_limit_bytes=LIMIT, dimension_semantics=("arbitrary",)
        ),
        cost_estimate=pl.CostEstimate(flops=flops, bytes_accessed=moved, transcendentals=0),
        name=name,
    )(*args)


def fixed(rows, columns):
    return pl.BlockSpec(
        (rows, columns), lambda i: (0, 0), pipeline_mode=pl.Buffered(buffer_count=1)
    )


def rows_of(rows, columns):
    return pl.BlockSpec((rows, columns), lambda i: (i, 0))


def owner_forward(rows, expander, reducer):
    def body(rows, expander, reducer, active_out, slope_out, parts_out):
        active, slope = gelu_pieces(dot(rows[...], expander[...]))
        active = active.astype(bf16)
        active_out[...] = active
        slope_out[...] = slope.astype(bf16)
        parts_out[...] = dot(active, reducer[...]).astype(bf16)

    block = rows_of(512, D)
    return grid_call(
        body,
        (2,),
        [block, fixed(D, D), fixed(D, D)],
        (shape(1024, D),) * 3,
        [block] * 3,
        [],
        (rows, expander, reducer),
        4300000000,
        12000000,
        "owner",
    )


def owner_backward(incoming, slope, expander, reducer):
    def body(incoming, slope, expander, reducer, grad_out, rows_out):
        grad = (dot_nt(incoming[...], reducer[...]) * slope[...].astype(f32)).astype(bf16)
        grad_out[...] = grad
        rows_out[...] = dot_nt(grad, expander[...]).astype(bf16)

    block = rows_of(256, D)
    return grid_call(
        body,
        (4,),
        [block, block, fixed(D, D), fixed(D, D)],
        (shape(1024, D),) * 2,
        [block] * 2,
        [],
        (incoming, slope, expander, reducer),
        4300000000,
        12000000,
        "owner_back",
    )


def places(kind):
    row = lax.broadcasted_iota(jnp.int32, (128, 256), 0)
    column = lax.broadcasted_iota(jnp.int32, (128, 256), 1)
    return (column == (row // 4) * 8 + kind * 4 + row % 4).astype(bf16)


def owner_both(arrived, expander, reducer):
    def body(arrived, expander, reducer, rows, grads, active_out, grad_out, sent):
        for block in range(2):
            packed = arrived[block * 256 : (block + 1) * 256, :]
            place = slice(block * 128, (block + 1) * 128)
            rows[place, :] = dot(places(0), packed).astype(bf16)
            grads[place, :] = dot(places(1), packed).astype(bf16)
        for low in range(0, 2048, 512):
            units = slice(low, low + 512)
            active, slope = gelu_pieces(dot(rows[...], expander[:, units]))
            active_out[:, units] = active.astype(bf16)
            grad_out[:, units] = (dot_nt(grads[...], reducer[units, :]) * slope).astype(bf16)
        parts = dot(active_out[...], reducer[...]).astype(bf16)
        returned = dot_nt(grad_out[...], expander[...]).astype(bf16)
        for block in range(2):
            place = slice(block * 128, (block + 1) * 128)
            sent[block * 256 : (block + 1) * 256, :] = (
                dot_tn(places(0), parts[place]) + dot_tn(places(1), returned[place])
            ).astype(bf16)

    return grid_call(
        body,
        (2,),
        [rows_of(512, D), fixed(D, 2048), fixed(2048, D)],
        (shape(512, D), shape(512, D), shape(512, 2048), shape(512, 2048), shape(1024, D)),
        [rows_of(256, D), rows_of(256, D), rows_of(256, 2048), rows_of(256, 2048), rows_of(512, D)],
        [],
        (arrived, expander, reducer),
        9000000000,
        20000000,
        "owner_both",
    )


def feed_both(blocks, weights):
    def body(
        block_a, block_b, block_c, block_d, weights, own, other, gradient, rows, active, grad
    ):
        part = pl.program_id(0)

        @pl.when(part == 0)
        def _():
            for i, block in enumerate((block_a, block_b, block_c, block_d)):
                rows[i * ROWS : (i + 1) * ROWS, :] = block[...]
            value, slope = gelu_pieces(dot(rows[:, 0:D], weights[:, 0:D]))
            active[...] = value.astype(bf16)
            back = dot_nt(rows[:, D : 2 * D], weights[:, D : 2 * D]) * slope
            grad[...] = back.astype(bf16)
            gradient[...] = dot_tn(rows[:, 0:D], grad[...]).astype(bf16)

        @pl.when(part == 1)
        def _():
            gradient[...] = dot_tn(active[...], rows[:, D : 2 * D]).astype(bf16)
            mine, twin = slice(0, 2 * ROWS), slice(2 * ROWS, 4 * ROWS)
            for place, out in ((twin, other), (mine, own)):
                out[:, 0:D] = dot(active[place, :], weights[:, D : 2 * D]).astype(out.dtype)
                out[:, D : 2 * D] = dot_nt(grad[place, :], weights[:, 0:D]).astype(out.dtype)

    full = fixed(ROWS, 2 * D)
    return pl.pallas_call(
        body,
        grid=(2,),
        in_specs=[full] * 4 + [fixed(D, 2 * D)],
        out_shape=(shape(2 * ROWS, 2 * D, dtype=f32), shape(2 * ROWS, 2 * D), shape(D, 4224)),
        out_specs=[
            pl.BlockSpec((2 * ROWS, 2 * D), lambda i: (0, 0)),
            pl.BlockSpec((2 * ROWS, 2 * D), lambda i: (0, 0)),
            pl.BlockSpec((D, D), lambda i: (0, i)),
        ],
        scratch_shapes=[
            pltpu.VMEM((4 * ROWS, 2 * D), bf16),
            pltpu.VMEM((4 * ROWS, D), bf16),
            pltpu.VMEM((4 * ROWS, D), bf16),
        ],
        compiler_params=pltpu.CompilerParams(
            vmem_limit_bytes=LIMIT, dimension_semantics=("arbitrary",)
        ),
        cost_estimate=pl.CostEstimate(
            flops=1000000, bytes_accessed=1000000, transcendentals=0
        ),
        name="feed",
    )(*blocks, weights)


def after(value, *others):
    return lax.optimization_barrier((value, *others))[0]


def gather_line(value):
    return jnp.concatenate(around(value), axis=0)


def scatter_column(other, own):
    got = swap(other)
    low = (own[ROWS:] + got[ROWS:].astype(f32)).astype(bf16)
    parts = (
        shift(low[:ROWS], "z", -1),
        shift(low[ROWS : 2 * ROWS], "z", 1),
        shift(low[2 * ROWS :], "z", 2),
    )
    return own[:ROWS] + got[:ROWS].astype(f32), parts


def around(value):
    return value, shift(value, "z", 1), shift(value, "z", -1), shift(value, "z", 2)


def positions(route):
    chosen = route[:, 0]
    row = jnp.arange(ROWS, dtype=jnp.int32)
    earlier = (row[None, :] < row[:, None]) & (row[None, :] // SEQ == row[:, None] // SEQ)
    same = (chosen[None, :] == chosen[:, None]) & earlier
    return chosen, row // SEQ, jnp.sum(same.astype(jnp.int32), axis=1)


def slots_first(route):
    chosen, sequence, position = positions(route)
    slot = chosen * 8 + sequence * 4 + position
    return slot[:, None], slot[None, :]


def slots_second(route):
    chosen, sequence, position = positions(route)
    slot = (chosen // 32) * 256 + (chosen % 32) * 8 + sequence * 2 + position
    return slot[:, None], slot[None, :]


def exchange(rows):
    blocks = rows.reshape(128, 8, rows.shape[-1])
    moved = lax.all_to_all(blocks, ALL, split_axis=0, concat_axis=0, tiled=True)
    return moved.reshape(rows.shape)


def exchange_plane(packed):
    blocks = packed.reshape(16, 64, packed.shape[1])
    return lax.all_to_all(blocks, PLANE, split_axis=0, concat_axis=0, tiled=True)


def add_blocks(blocks):
    return jnp.sum(blocks.astype(f32), axis=0).astype(bf16)


def pack_attention(inner, outer, mixer, gain, regain):
    blank = jnp.zeros((inner.shape[0], 124), bf16)
    return jnp.concatenate([inner, outer, mixer, gain[:, None], regain[:, None], blank], axis=1)


def pack_feed_first(widen, narrow):
    z, c = lax.axis_index("z"), lax.axis_index("c")
    units = widen.reshape(32, 16, 2, 4, 32)
    units = lax.dynamic_index_in_dim(units, z, 3, keepdims=False)
    mine = lax.dynamic_index_in_dim(units, c, 2, keepdims=False).reshape(32, 512)
    other = lax.dynamic_index_in_dim(units, 1 - c, 2, keepdims=False).reshape(32, 512)
    columns = in_order(c, mine, swap(other), 1)
    rows = lax.dynamic_slice_in_dim(narrow, z * 32, 32, 0)
    return jnp.concatenate([columns, rows], axis=0)


def pack_feed_second(widen, narrow):
    z, c = lax.axis_index("z"), lax.axis_index("c")
    half = lax.rem(z, 2)
    units = widen.reshape(32, 16, 2, 2, 64)
    units = lax.dynamic_index_in_dim(units, half, 3, keepdims=False)
    mine = lax.dynamic_index_in_dim(units, c, 2, keepdims=False).reshape(32, 1024)
    other = lax.dynamic_index_in_dim(units, 1 - c, 2, keepdims=False).reshape(32, 1024)
    columns = in_order(c, mine, swap(other), 0)
    return jnp.concatenate([columns, half_of(narrow, half, 0)], axis=1)


def quarter(place, i):
    return lax.rem(place[0] + (0, 3, 1, 2)[i], 4)


def finish_second(place, summed):
    c = lax.axis_index("c")
    rows = lax.dynamic_slice_in_dim(summed, 32 * (1 - c), 32, 1)
    got = swap(jnp.concatenate([rows[:, :, :1024], rows[:, :, 2048:]], axis=2))

    def body(place, summed, got, widen, narrow, inner, outer, few):
        first = lax.broadcasted_iota(jnp.int32, (32, 128), 1) < 64
        rows = pl.ds(pl.multiple_of(place[1] * 32, 32), 32)

        def mine(z, low, size):
            return summed[z, rows, low : low + size].astype(f32)

        def twin(z, low, size):
            low = low if low < 1024 else low - 1024
            return got[z, :, low : low + size].astype(f32)

        for core, term in ((place[1], mine), (1 - place[1], twin)):
            for low in range(0, 1024, 128):
                one = term(0, low, 128) + term(2, low, 128)
                two = term(1, low, 128) + term(3, low, 128)
                even = jnp.where(first, one, pltpu.roll(two, 64, 1))
                odd = jnp.where(first, pltpu.roll(one, 64, 1), two)
                for i, value in ((0, even), (1, odd)):
                    column = pl.multiple_of((low // 64 + i) * 256 + core * 128, 128)
                    widen[:, pl.ds(column, 128)] = value
            for out, low, size in ((inner, 2048, 1536), (outer, 3584, 512)):
                total = (term(0, low, size) + term(1, low, size)) + (
                    term(2, low, size) + term(3, low, size)
                )
                out[:, pl.ds(pl.multiple_of(core * size, 128), size)] = total
        total = jnp.zeros((32, 128), f32)
        for z in range(4):
            total += mine(z, 4096, 128) + twin(z, 4096, 128)
        few[...] = total
        for half in range(2):
            narrow[half * 64 : half * 64 + 64, :] = summed[half, :, 1024:2048].astype(f32) + summed[
                half + 2, :, 1024:2048
            ].astype(f32)

    outs = (
        shape(32, 4096, dtype=f32),
        shape(ROWS, D, dtype=f32),
        shape(32, 3072, dtype=f32),
        shape(32, D, dtype=f32),
        shape(32, 128, dtype=f32),
    )
    widen, narrow, inner, outer, few = call(
        body, outs, (place, summed, got), 1000000, 1000000, name="second_out"
    )
    return (widen, narrow), (inner, outer), (few[:, 0:2], few[:, 2], few[:, 3])


def finish_feed_first(place, blocks):
    c = lax.axis_index("c")
    summed = add_blocks(blocks)
    widen = summed[:, :512]
    widen = in_order(c, half_of(widen, c, 0), swap(half_of(widen, 1 - c, 0)), 1)
    narrow = jnp.concatenate([summed[:32, 512:], summed[32:, 512:]], axis=1)
    pieces = around(jnp.concatenate([widen, narrow], axis=0))

    def body(place, own, before, later, opposite, widen, narrow):
        lane = lax.broadcasted_iota(jnp.int32, (32, 128), 1) // 32
        for i, source in enumerate((own, before, later, opposite)):
            z = quarter(place, i)
            narrow[pl.ds(pl.multiple_of(z * 32, 32), 32), :] = source[32:64, :].astype(f32)
            for core in range(2):
                for four in range(4):
                    column = core * 512 + four * 128
                    value = source[0:32, column : column + 128].astype(f32)
                    for k in range(4):
                        moved = pltpu.roll(value, lax.rem(z * 32 + (128 - k * 32), 128), 1)
                        low = (four * 4 + k) * 256 + core * 128
                        out = widen.at[:, low : low + 128]
                        if i == 0:
                            out[...] = moved
                        else:
                            out[...] = jnp.where(lane == z, moved, out[...])

    outs = (shape(32, 4096, dtype=f32), shape(ROWS, D, dtype=f32))
    return call(body, outs, (place, *pieces), 1000000, 1000000, name="feed_one_out")


def finish_attention_first(place, blocks):
    c = lax.axis_index("c")
    summed = add_blocks(blocks)
    mine, got = half_of(summed, c, 0), swap(half_of(summed, 1 - c, 0))
    pieces = around(in_order(c, mine, got, 1))

    def body(place, own, before, later, opposite, inner, outer, few):
        total = (own[:, 512:640].astype(f32) + opposite[:, 512:640].astype(f32)) + (
            before[:, 512:640].astype(f32) + later[:, 512:640].astype(f32)
        )
        twin = (own[:, 1152:1280].astype(f32) + opposite[:, 1152:1280].astype(f32)) + (
            before[:, 1152:1280].astype(f32) + later[:, 1152:1280].astype(f32)
        )
        few[...] = total + twin
        for i, source in enumerate((own, before, later, opposite)):
            z = quarter(place, i)
            for core in range(2):
                low = core * 640
                index = z * 2 + core
                inner[:, pl.ds(pl.multiple_of(index * 384, 128), 384)] = source[
                    :, low : low + 384
                ].astype(f32)
                outer[:, pl.ds(pl.multiple_of(index * 128, 128), 128)] = source[
                    :, low + 384 : low + 512
                ].astype(f32)

    outs = (shape(32, 3072, dtype=f32), shape(32, D, dtype=f32), shape(32, 128, dtype=f32))
    inner, outer, few = call(body, outs, (place, *pieces), 1000000, 1000000, name="attention_out")
    return inner, outer, few[:, 0:2], few[:, 2], few[:, 3]


def on_device(
    tokens,
    cotangent,
    routes_first,
    routes_second,
    inner_first,
    outer_first,
    widen_first,
    narrow_first,
    mixer_first,
    gain_first,
    regain_first,
    inner_second,
    outer_second,
    widen_second,
    narrow_second,
    mixer_second,
    gain_second,
    regain_second,
    expand_first,
    reduce_first,
    expand_second,
    reduce_second,
):
    place = jnp.stack([lax.axis_index("z"), lax.axis_index("c")]).astype(jnp.int32)
    gathered = lax.all_gather(
        jnp.concatenate(
            [
                pack_attention(inner_first, outer_first, mixer_first, gain_first, regain_first),
                pack_attention(inner_second, outer_second, mixer_second, gain_second, regain_second),
            ],
            axis=1,
        ),
        ("x", "y", "c"),
        axis=0,
        tiled=True,
    )
    gathered_feed_first = lax.all_gather(
        pack_feed_first(widen_first, narrow_first), PLANE, axis=0, tiled=True
    )
    gathered_feed = lax.all_gather(
        pack_feed_second(widen_second, narrow_second), PLANE, axis=0, tiled=True
    )
    column_first, row_first = slots_first(routes_first)
    column_second, row_second = slots_second(routes_second)
    expander, reducer = expand_first[0], reduce_first[0]

    pair, joint, middle, normed_two, shares, send = first_front(tokens, gathered, row_first)
    received = exchange(send)
    group = gather_line(normed_two)
    received = after(received, group)
    active, slope, parts = owner_forward(received, expander, reducer)
    back = exchange(parts)
    group_twin = swap(group)
    other, own, active_feed, slope_feed, widen_one, narrow_one = feed_forward(
        group, group_twin, gathered_feed_first
    )
    dense_own, dense_parts = scatter_column(other, own)

    output, stream, dense, expert, pair_s, joint_s, middle_s, feed_s, shares_s, send = second_front(
        back,
        column_first,
        middle,
        shares,
        dense_own,
        dense_parts,
        cotangent,
        gathered,
        row_second,
    )
    arrived = exchange(send)
    feed_flipped = flip(feed_s)
    feed_blocks = (feed_s, feed_flipped, swap(feed_s), swap(feed_flipped))
    arrived = after(arrived, *feed_blocks)
    line = lax.all_gather(after(pair, arrived), COLUMN, axis=0, tiled=True)
    rows, incoming_s, active_s, grad_s, sent = owner_both(
        arrived, expand_second[0], reduce_second[0]
    )
    back = exchange(sent)
    feed_blocks = lax.optimization_barrier((*feed_blocks, sent))[:4]
    terms, terms_twin, feed_gradient = feed_both(feed_blocks, gathered_feed)
    got = swap(terms_twin)
    flipped = flip((terms[ROWS:] + got[ROWS:].astype(f32)).astype(bf16))
    pair_twin = swap(pair_s)
    back = after(back, line, pair_twin)
    output_two, upstream, mine, other, small, grad_dense, send = second_back(
        place,
        back,
        column_second,
        cotangent,
        middle_s,
        shares_s,
        terms,
        got,
        flipped,
        feed_s,
        joint_s,
        stream,
        gathered,
        shares,
        row_first,
    )
    grad_s = after(grad_s, send)
    grad_expand_two = dot_tn(rows, grad_s)
    grad_reduce_two = dot_tn(active_s, after(incoming_s, send))

    incoming = after(exchange(send), grad_expand_two, grad_reduce_two)
    grad_group = gather_line(grad_dense)
    grad_group_twin = swap(grad_group)
    feed_other, feed_own, grad_hidden = feed_backward(
        grad_group, grad_group_twin, slope_feed, widen_one, narrow_one
    )
    packed = weights_second(feed_gradient, pair_s, pair_twin, mine, swap(other), small)
    packed = lax.psum_scatter(packed, PLANE, scatter_dimension=0, tiled=True)
    grad_first, grad_rows = owner_backward(incoming, slope, expander, reducer)
    back = exchange(grad_rows)
    feed_own, feed_parts = scatter_column(feed_other, feed_own)
    feed_packed = weights_feed(
        group, group_twin, grad_hidden, active_feed, grad_group, grad_group_twin
    )
    back = after(back, feed_packed)
    feed_sums = exchange_plane(after(feed_packed, back))
    gradient_tokens, mine, other, small = first_back(
        place,
        back,
        column_first,
        upstream,
        middle,
        shares,
        dense,
        expert,
        feed_own,
        feed_parts,
        normed_two,
        joint,
        tokens,
        gathered,
    )
    got = swap(other)
    ahead = [jnp.concatenate([mine[i], got[i]], axis=0) for i in (1, 2, 3)]
    parts = (shift(ahead[0], "z", 1), shift(ahead[1], "z", -1), shift(ahead[2], "z", 2))
    packed = lax.all_gather(after(packed, mine), "z", axis=0)
    grad_first = after(grad_first, mine)
    grad_expand_one = dot_tn(received, grad_first)
    grad_reduce_one = dot_tn(active, after(incoming, mine))
    first_packed = weights_first(place, line, mine, got, parts, small)
    first_packed = after(first_packed, feed_sums)
    blocks = exchange_plane(first_packed)
    feed_finals = finish_feed_first(place, feed_sums)
    feed_finals_second, finals_second, few_second = finish_second(place, packed)
    blocks = after(
        blocks, feed_finals, feed_finals_second, finals_second, grad_expand_one, grad_reduce_one
    )
    inner, outer, *few_first = finish_attention_first(place, blocks)
    return (
        (output, output_two, gradient_tokens)
        + (inner, outer)
        + tuple(feed_finals)
        + tuple(few_first)
        + finals_second
        + tuple(feed_finals_second)
        + few_second
        + (
            grad_expand_one[None],
            grad_reduce_one[None],
            grad_expand_two[None],
            grad_reduce_two[None],
        )
    )


def solution(mesh):
    fine = Mesh(mesh.devices.reshape(4, 4, 4, 2), ALL)
    owner = ("x", "y", "c")
    tokens = P(ALL, None)
    dense = (P(owner, None),) * 5 + (P(owner),) * 2
    experts = (
        P(owner, None, "z"),
        P(owner, "z", None),
        P(ALL, None, None),
        P(ALL, None, None),
    )
    return jax.shard_map(
        on_device,
        mesh=fine,
        in_specs=(tokens,) * 4 + dense + dense + experts,
        out_specs=(tokens,) * 3 + dense + dense + experts,
        check_vma=False,
    )
```

```python
import jax
import jax.numpy as jnp
from jax import lax
from jax.experimental import pallas as pl
from jax.experimental.pallas import tpu as pltpu
from jax.sharding import Mesh, PartitionSpec as P

HEADS = 16
HEAD = 64
SEQ = 64
ROWS = 128
D = 1024
PACKED = 4224
SCALE = HEAD**-0.5
ALL = ("z", "x", "y", "c")
PLANE = ("x", "y")
COLUMN = ("z", "c")
SIZES = {"z": 4, "x": 4, "y": 4, "c": 2}
epsilon = 1e-05
bf16 = jnp.bfloat16
f32 = jnp.float32
LIMIT = 56 * 1024 * 1024


def shift(value, axis, step):
    size = SIZES[axis]
    return lax.ppermute(value, axis, [(i, (i + step) % size) for i in range(size)])


def swap(value):
    return shift(value, "c", 1)


def flip(value):
    return lax.ppermute(value, "z", [(0, 1), (1, 0), (2, 3), (3, 2)])


def dot(a, b):
    return jnp.dot(a, b, preferred_element_type=f32)


def dot_tn(a, b):
    return lax.dot_general(a, b, (((0,), (0,)), ((), ())), preferred_element_type=f32)


def dot_nt(a, b):
    return lax.dot_general(a, b, (((1,), (1,)), ((), ())), preferred_element_type=f32)


def in_order(core, mine, twin, axis):
    return jnp.where(
        core == 0,
        jnp.concatenate([mine, twin], axis=axis),
        jnp.concatenate([twin, mine], axis=axis),
    )


def half_of(value, which, axis):
    size = value.shape[axis] // 2
    return lax.dynamic_slice_in_dim(value, which * size, size, axis)


def shape(*dims, dtype=bf16):
    return jax.ShapeDtypeStruct(dims, dtype)


def whole():
    return pl.BlockSpec(memory_space=pltpu.VMEM)


def space_of(value):
    if value.dtype == jnp.int32 and value.ndim == 1:
        return pl.BlockSpec(memory_space=pltpu.SMEM)
    return whole()


def call(body, outs, args, flops, moved, far=(), scratch=(), name=None):
    return pl.pallas_call(
        body,
        out_shape=outs,
        in_specs=[
            pl.BlockSpec(memory_space=pl.ANY) if i in far else space_of(arg)
            for i, arg in enumerate(args)
        ],
        out_specs=[whole()] * len(outs),
        scratch_shapes=list(scratch),
        compiler_params=pltpu.CompilerParams(vmem_limit_bytes=LIMIT),
        cost_estimate=pl.CostEstimate(flops=flops, bytes_accessed=moved, transcendentals=0),
        name=name,
    )(*args)


def start_weights(far, near, sems):
    copies = []
    for i, low, high in ((4, 4096, 4224), (0, 0, D), (1, D, 2 * D), (2, 2 * D, 3 * D), (3, 3 * D, 4096)):
        copy = pltpu.make_async_copy(
            far.at[:, low:high], near.at[:, low:high], sems.at[i]
        )
        copy.start()
        copies.append(copy)
    return copies


WEIGHTS = (pltpu.VMEM((D, PACKED), bf16), pltpu.SemaphoreType.DMA((5,)))


def vector_rows(near):
    pick = lax.broadcasted_iota(jnp.int32, (8, 128), 0) == lax.broadcasted_iota(
        jnp.int32, (8, 128), 1
    )
    return dot_nt(pick.astype(bf16), near[:, 4096:4224])


def normalize(values):
    center = values - jnp.mean(values, axis=-1, keepdims=True)
    spread = jnp.mean(center * center, axis=-1, keepdims=True)
    inverse = lax.rsqrt(spread + epsilon)
    return center * inverse, inverse


def normalize_backward(hat, inverse, gradient):
    return inverse * (
        gradient
        - jnp.mean(gradient, axis=-1, keepdims=True)
        - hat * jnp.mean(gradient * hat, axis=-1, keepdims=True)
    )


def lane_half(rows=ROWS):
    return lax.broadcasted_iota(jnp.int32, (rows, 128), 1) < HEAD


def split_heads(pair):
    first = lane_half()
    blank = jnp.zeros_like(pair)
    return jnp.concatenate([jnp.where(first, pair, blank), jnp.where(first, blank, pair)], axis=0)


def own_sequence(table):
    first = lane_half(SEQ)
    return [
        jnp.where(first, table[low : low + SEQ], table[low + SEQ : low + 2 * SEQ])
        for low in (0, ROWS)
    ]


def spread_sequences(blocks):
    first = lane_half(SEQ)
    parts = []
    for block in blocks:
        parts += [jnp.where(first, block, 0.0), jnp.where(first, 0.0, block)]
    return jnp.concatenate(parts, axis=0).astype(bf16)


def attention_of(query, keys):
    key = lax.broadcasted_iota(jnp.int32, (SEQ, ROWS), 0)
    place = jnp.bitwise_and(lax.broadcasted_iota(jnp.int32, (SEQ, ROWS), 1), SEQ - 1)
    result = []
    for scores in own_sequence(dot_nt(split_heads(keys), query) * SCALE):
        scores = jnp.where(key <= place, scores, -1e30)
        raised = jnp.exp(scores - jnp.max(scores, axis=0, keepdims=True))
        result.append(raised / jnp.sum(raised, axis=0, keepdims=True))
    return result


def pair_of(ref, part, pair):
    return ref[:, pl.ds(pl.multiple_of(part * D + pair * 128, 128), 128)]


def front(stream, near, copies, normed_out, joint_out, mixed_out, middle_out, two_out, share_out):
    copies[0].wait()
    vectors = vector_rows(near)
    hat, _ = normalize(stream)
    normed = (hat * vectors[2:3]).astype(bf16)
    normed_out[...] = normed
    for part in range(3):
        copies[part + 1].wait()
        for low in range(part * D, part * D + D, 512):
            joint_out[:, low : low + 512] = dot(normed, near[:, low : low + 512]).astype(bf16)

    @pl.loop(0, HEADS // 2, unroll=True)
    def _(pair):
        query, keys, values = (pair_of(joint_out, part, pair) for part in range(3))
        table = spread_sequences(attention_of(query, keys))
        one = dot_tn(table[0:ROWS], values)
        two = dot_tn(table[ROWS : 2 * ROWS], values)
        column = pl.ds(pl.multiple_of(pair * 128, 128), 128)
        mixed_out[:, column] = jnp.where(lane_half(), one, two).astype(bf16)

    mixed = mixed_out[...]
    copies[4].wait()
    for low in range(0, D, 512):
        middle_out[:, low : low + 512] = stream[:, low : low + 512] + dot(
            mixed, near[:, 3072 + low : 3072 + low + 512]
        )
    hat, _ = normalize(middle_out[...])
    normed_two = (hat * vectors[3:4]).astype(bf16)
    two_out[...] = normed_two
    logits = dot(normed_two, near[:, 4096:4224])
    one, two = logits[:, 0:1], logits[:, 1:2]
    top = jnp.maximum(one, two)
    one, two = jnp.exp(one - top), jnp.exp(two - top)
    total = one + two
    one, two = one / total, two / total
    lane = lax.broadcasted_iota(jnp.int32, (ROWS, 128), 1)
    share_out[...] = jnp.where(lane == 0, one, two)
    return normed_two, one, two


def send_first(rows, slot_row, out):
    slots = lax.broadcasted_iota(jnp.int32, (256, ROWS), 0)
    table = (slots == slot_row[...]).astype(bf16)
    buffer = dot(table, rows).astype(bf16)
    for z in range(4):
        out[z * 256 : (z + 1) * 256, :] = buffer


def send_second(rows, grads, slot_row, out):
    slots = lax.broadcasted_iota(jnp.int32, (256, ROWS), 0)
    for group in range(2):
        wanted = slot_row[...] - group * 256
        buffer = dot((slots == wanted).astype(bf16), rows) + dot(
            (slots == wanted + 4).astype(bf16), grads
        )
        buffer = buffer.astype(bf16)
        for z in (2 * group, 2 * group + 1):
            out[z * 256 : (z + 1) * 256, :] = buffer


def take_first(back, slot_column):
    column = lax.broadcasted_iota(jnp.int32, (ROWS, 1024), 1)
    table = (slot_column[...] == jnp.bitwise_and(column, 255)).astype(bf16)
    return dot(table, back[...])


def take_second(back, slot_column):
    column = lax.broadcasted_iota(jnp.int32, (ROWS, 1024), 1)
    place = jnp.where(column >= 512, 256, 0) + jnp.bitwise_and(column, 255)
    rows = dot((slot_column[...] == place).astype(bf16), back[...])
    grads = dot((slot_column[...] + 4 == place).astype(bf16), back[...])
    return rows, grads


def backward(
    stream,
    near,
    copies,
    joint_ref,
    middle,
    normed_two,
    one,
    two,
    upstream,
    dense,
    expert,
    incoming,
    joint_out,
    attended_out,
    small_out,
    mixed_ref,
):
    copies[0].wait()
    vectors = vector_rows(near)
    first = jnp.sum(upstream * dense, axis=1, keepdims=True)
    second = jnp.sum(upstream * expert, axis=1, keepdims=True)
    both = one * first + two * second
    first, second = one * (first - both), two * (second - both)
    normed_two = normed_two.astype(f32)
    gradient = first * vectors[0:1] + second * vectors[1:2] + incoming
    hat, inverse = normalize(middle)
    small_out[0:1, :] = jnp.sum(normed_two * first, axis=0, keepdims=True)
    small_out[1:2, :] = jnp.sum(normed_two * second, axis=0, keepdims=True)
    small_out[3:4, :] = jnp.sum(gradient * hat, axis=0, keepdims=True)
    small_out[4:8, :] = jnp.zeros((4, D), f32)
    grad_middle = upstream + normalize_backward(hat, inverse, gradient * vectors[3:4])
    attended = grad_middle.astype(bf16)
    attended_out[...] = attended
    copies[4].wait()
    for low in range(0, D, 512):
        mixed_ref[:, low : low + 512] = dot_nt(attended, near[low : low + 512, 3072:4096]).astype(
            bf16
        )

    @pl.loop(0, HEADS // 2, unroll=True)
    def _(pair):
        query, keys, values = (pair_of(joint_ref, part, pair) for part in range(3))
        column = pl.ds(pl.multiple_of(pair * 128, 128), 128)
        grad_mixed = mixed_ref[:, column]
        attention = attention_of(query, keys)
        grad_attention = own_sequence(dot_nt(split_heads(values), grad_mixed))
        grad_scores = [
            weight * (grad - jnp.sum(weight * grad, axis=0, keepdims=True))
            for weight, grad in zip(attention, grad_attention)
        ]
        grad_scores = spread_sequences(grad_scores)
        grad_keys = dot(grad_scores, query) * SCALE
        grad_values = dot(spread_sequences(attention), grad_mixed)
        halves = (
            (
                dot_tn(grad_scores[0:ROWS], keys) * SCALE,
                dot_tn(grad_scores[ROWS : 2 * ROWS], keys) * SCALE,
            ),
            (grad_keys[0:ROWS], grad_keys[ROWS : 2 * ROWS]),
            (grad_values[0:ROWS], grad_values[ROWS : 2 * ROWS]),
        )
        for part in range(3):
            place = pl.ds(pl.multiple_of(part * D + pair * 128, 128), 128)
            joint_out[:, place] = jnp.where(lane_half(), *halves[part]).astype(bf16)

    for copy in copies[1:4]:
        copy.wait()
    parts = []
    for low in range(0, D, 256):
        parts.append(dot_nt(joint_out[...], near[low : low + 256, 0:3072]))
    grad_normed = jnp.concatenate(parts, axis=1)
    hat, inverse = normalize(stream)
    small_out[2:3, :] = jnp.sum(grad_normed * hat, axis=0, keepdims=True)
    return grad_middle + normalize_backward(hat, inverse, grad_normed * vectors[2:3])


def halves_of(pair):
    return pair.at[:, 0:D], pair.at[:, D : 2 * D]


def first_front(tokens, weights, slot_row):
    def body(tokens, far, slot_row, pair, joint, middle, two, shares, send, near, sems):
        copies = start_weights(far, near, sems)
        normed, mixed = halves_of(pair)
        rows, _, _ = front(
            tokens[...].astype(f32), near, copies, normed, joint, mixed, middle, two, shares
        )
        send_first(rows, slot_row, send)

    outs = (
        shape(ROWS, 2 * D),
        shape(ROWS, 3 * D),
        shape(ROWS, D, dtype=f32),
        shape(ROWS, D),
        shape(ROWS, 128, dtype=f32),
        shape(1024, D),
    )
    args = (tokens, weights, slot_row)
    return call(body, outs, args, 1300000000, 14000000, far=(1,), scratch=WEIGHTS, name="front")


def second_front(back, slot_column, middle, shares, own, parts, cotangent, weights, slot_row):
    def body(
        back,
        slot_column,
        middle,
        shares,
        own,
        part_a,
        part_b,
        part_c,
        cotangent,
        far,
        slot_row,
        low_out,
        stream_out,
        dense_out,
        expert_out,
        pair,
        joint,
        middle_out,
        feed,
        shares_out,
        send,
        near,
        sems,
    ):
        copies = start_weights(far, near, sems)
        expert = take_first(back, slot_column)
        dense = own[...] + part_a[...].astype(f32) + part_b[...].astype(f32) + part_c[...].astype(f32)
        dense_out[...] = dense
        expert_out[...] = expert
        stream = middle[...] + shares[:, 0:1] * dense + shares[:, 1:2] * expert
        stream_out[...] = stream
        low_out[...] = stream.astype(bf16)
        normed, mixed = halves_of(pair)
        two, grad_dense = halves_of(feed)
        rows, one, other = front(
            stream, near, copies, normed, joint, mixed, middle_out, two, shares_out
        )
        upstream = cotangent[...].astype(f32)
        grad_dense[...] = (upstream * one).astype(bf16)
        send_second(rows, (upstream * other).astype(bf16), slot_row, send)

    outs = (
        shape(ROWS, D),
        shape(ROWS, D, dtype=f32),
        shape(ROWS, D, dtype=f32),
        shape(ROWS, D, dtype=f32),
        shape(ROWS, 2 * D),
        shape(ROWS, 3 * D),
        shape(ROWS, D, dtype=f32),
        shape(ROWS, 2 * D),
        shape(ROWS, 128, dtype=f32),
        shape(1024, D),
    )
    args = (back, slot_column, middle, shares, own, *parts, cotangent, weights, slot_row)
    return call(body, outs, args, 1800000000, 20000000, far=(9,), scratch=WEIGHTS, name="between")


BACK = WEIGHTS + (
    pltpu.VMEM((ROWS, D), bf16),
    pltpu.VMEM((ROWS, 3 * D), bf16),
    pltpu.VMEM((ROWS, D), bf16),
)


def second_back(
    place,
    back,
    slot_column,
    cotangent,
    middle,
    shares,
    own,
    flipped,
    feed,
    joint,
    stream,
    weights,
    first_shares,
    slot_row,
):
    def body(
        place,
        back,
        slot_column,
        cotangent,
        middle,
        shares,
        own,
        flipped,
        feed,
        joint,
        stream,
        far,
        first_shares,
        slot_row,
        low_out,
        grad_out,
        mine,
        other,
        small_out,
        grad_dense,
        send,
        near,
        sems,
        mixed,
        joint_grad,
        attended,
    ):
        copies = start_weights(far, near, sems)
        expert, from_experts = take_second(back, slot_column)
        total = own[...] + flipped[...].astype(f32)
        dense, from_feed = total[:, 0:D], total[:, D : 2 * D]
        one, two = shares[:, 0:1], shares[:, 1:2]
        low_out[...] = (middle[...] + one * dense + two * expert).astype(bf16)
        gradient = backward(
            stream[...],
            near,
            copies,
            joint,
            middle[...],
            feed[:, 0:D],
            one,
            two,
            cotangent[...].astype(f32),
            dense,
            expert,
            from_feed + from_experts,
            joint_grad,
            attended,
            small_out,
            mixed,
        )
        grad_out[...] = gradient
        grad_dense[...] = (gradient * first_shares[:, 0:1]).astype(bf16)
        send_first((gradient * first_shares[:, 1:2]).astype(bf16), slot_row, send)
        for out, core in ((mine, place[1]), (other, 1 - place[1])):
            wide = pl.multiple_of(core * 1536, 128)
            out[:, 0:1536] = joint_grad[:, pl.ds(wide, 1536)]
            out[:, 1536:2048] = attended[:, pl.ds(pl.multiple_of(core * 512, 128), 512)]

    outs = (
        shape(ROWS, D),
        shape(ROWS, D, dtype=f32),
        shape(ROWS, 2048),
        shape(ROWS, 2048),
        shape(8, D, dtype=f32),
        shape(ROWS, D),
        shape(1024, D),
    )
    args = (
        place,
        back,
        slot_column,
        cotangent,
        middle,
        shares,
        own,
        flipped,
        feed,
        joint,
        stream,
        weights,
        first_shares,
        slot_row,
    )
    return call(body, outs, args, 1000000, 1000000, far=(11,), scratch=BACK, name="turn")


def first_back(
    place, back, slot_column, upstream, middle, shares, dense, expert, own, parts, normed_two, joint, tokens, weights
):
    def body(
        place,
        back,
        slot_column,
        upstream,
        middle,
        shares,
        dense,
        expert,
        own,
        part_a,
        part_b,
        part_c,
        normed_two,
        joint,
        tokens,
        far,
        grad_out,
        mine,
        other,
        small_out,
        near,
        sems,
        mixed,
        joint_grad,
        attended,
    ):
        copies = start_weights(far, near, sems)
        incoming = take_first(back, slot_column)
        incoming = (
            own[...]
            + part_a[...].astype(f32)
            + part_b[...].astype(f32)
            + part_c[...].astype(f32)
            + incoming
        )
        grad_out[...] = backward(
            tokens[...].astype(f32),
            near,
            copies,
            joint,
            middle[...],
            normed_two[...],
            shares[:, 0:1],
            shares[:, 1:2],
            upstream[...],
            dense[...],
            expert[...],
            incoming,
            joint_grad,
            attended,
            small_out,
            mixed,
        )
        for out, core in ((mine, place[1]), (other, 1 - place[1])):
            for i, step in enumerate((0, 1, 3, 2)):
                index = lax.rem(place[0] + step, 4) * 2 + core
                wide = pl.ds(pl.multiple_of(index * 384, 128), 384)
                out[i, :, 0:384] = joint_grad[:, wide]
                out[i, :, 384:512] = attended[:, pl.ds(pl.multiple_of(index * 128, 128), 128)]

    outs = (
        shape(ROWS, D, dtype=f32),
        shape(4, ROWS, 512),
        shape(4, ROWS, 512),
        shape(8, D, dtype=f32),
    )
    args = (
        place,
        back,
        slot_column,
        upstream,
        middle,
        shares,
        dense,
        expert,
        own,
        *parts,
        normed_two,
        joint,
        tokens,
        weights,
    )
    return call(body, outs, args, 1000000, 1000000, far=(15,), scratch=BACK, name="back")


def few_columns(small):
    pick = lax.broadcasted_iota(jnp.int32, (8, 128), 0) == lax.broadcasted_iota(
        jnp.int32, (8, 128), 1
    )
    return dot_tn(small[...].astype(bf16), pick.astype(bf16)).astype(bf16)


def weights_first(place, line, mine, got, parts, small):
    def body(place, line, mine, got, part_a, part_b, part_c, small, out, ordered):
        def put(step, core, value):
            index = lax.rem(place[0] + step, 4) * 2 + core
            ordered[pl.ds(pl.multiple_of(index * ROWS, ROWS), ROWS), :] = value

        own, other = place[1], 1 - place[1]
        put(0, own, mine[0])
        put(0, other, got[0])
        for step, part in ((3, part_a), (1, part_b), (2, part_c)):
            put(step, own, part[0:ROWS, :])
            put(step, other, part[ROWS : 2 * ROWS, :])
        for low in range(0, D, 256):
            rows = slice(low, low + 256)
            for left, first, last in ((low, 0, 384), (D + low, 384, 512)):
                out[rows, first:last] = dot_tn(
                    line[:, left : left + 256], ordered[:, first:last]
                ).astype(bf16)
        out[:, 512:640] = few_columns(small)

    args = (place, line, mine, got, *parts, small)
    return call(
        body,
        (shape(D, 640),),
        args,
        1000000,
        1000000,
        scratch=(pltpu.VMEM((1024, 512), bf16),),
        name="first_weights",
    )[0]


def weights_second(packed, pair, pair_twin, mine, got, small):
    def body(packed, pair, pair_twin, mine, got, small, out, near, sem):
        for low in range(0, D, 256):
            rows = slice(low, low + 256)
            for left, first, last in ((low, 0, 1536), (D + low, 1536, 2048)):
                near[rows, first:last] = (
                    dot_tn(pair[:, left : left + 256], mine[:, first:last])
                    + dot_tn(pair_twin[:, left : left + 256], got[:, first:last])
                ).astype(bf16)
        near[:, 2048:2176] = few_columns(small)
        copy = pltpu.make_async_copy(near, out.at[:, 2048:4224], sem)
        copy.start()
        copy.wait()

    args = (packed, pair, pair_twin, mine, got, small)
    return pl.pallas_call(
        body,
        out_shape=shape(D, 4224),
        in_specs=[pl.BlockSpec(memory_space=pl.ANY)] + [whole()] * 5,
        out_specs=pl.BlockSpec(memory_space=pl.ANY),
        scratch_shapes=[pltpu.VMEM((D, 2176), bf16), pltpu.SemaphoreType.DMA(())],
        input_output_aliases={0: 0},
        compiler_params=pltpu.CompilerParams(vmem_limit_bytes=LIMIT),
        cost_estimate=pl.CostEstimate(flops=1000000, bytes_accessed=1000000, transcendentals=0),
        name="second_weights",
    )(*args)


def weights_feed(place, group, group_twin, grad_hidden, active, got, inc, inc_twin):
    def body(place, group, group_twin, grad_hidden, active, got, inc, inc_twin, out):
        base = place[1] * 512
        grad = grad_hidden[:, pl.ds(pl.multiple_of(base, 128), 512)]
        for low in range(0, D, 256):
            rows = slice(low, low + 256)
            out[rows, 0:512] = (
                dot_tn(group[:, rows], grad) + dot_tn(group_twin[:, rows], got[:, 0:512])
            ).astype(bf16)
        for low in range(0, 512, 256):
            units = active[:, pl.ds(pl.multiple_of(base + low, 128), 256)]
            narrow = (
                dot_tn(units, inc[...]) + dot_tn(got[:, 512 + low : 768 + low], inc_twin[...])
            ).astype(bf16)
            for i in range(8):
                start = low * 2 + i * 64
                part = narrow[i * 32 : (i + 1) * 32, :]
                out[start : start + 32, 512:1024] = part[:, 0:512]
                out[start + 32 : start + 64, 512:1024] = part[:, 512:1024]

    args = (place, group, group_twin, grad_hidden, active, got, inc, inc_twin)
    return call(body, (shape(D, 1024),), args, 1000000, 1000000, name="feed_weights")[0]


def feed_forward(group, packed):
    def body(group, far, own, part_a, part_b, part_c, active_out, slope_out, narrow, near, sem):
        copy = pltpu.make_async_copy(far.at[:, PACKED : PACKED + 2 * D], near, sem)
        copy.start()
        copy.wait()
        for i in range(16):
            for core in range(2):
                source = (i * 2 + core) * 32
                target = core * 512 + i * 32
                narrow[target : target + 32, :] = near[source : source + 32, D : 2 * D]
        for low in range(0, 512, 256):
            place = slice(low, low + 256)
            active, slope = gelu_pieces(dot(group[place, :], near[:, 0:D]))
            active = active.astype(bf16)
            active_out[place, :] = active
            slope_out[place, :] = slope.astype(bf16)
            terms = dot(active, narrow[...])
            first, second = ((own, part_a), (part_b, part_c))[low // 256]
            first[...] = terms[0:ROWS].astype(first.dtype)
            second[...] = terms[ROWS : 2 * ROWS].astype(bf16)

    outs = (
        shape(ROWS, D, dtype=f32),
        shape(ROWS, D),
        shape(ROWS, D),
        shape(ROWS, D),
        shape(512, D),
        shape(512, D),
        shape(D, D),
    )
    scratch = (pltpu.VMEM((D, 2 * D), bf16), pltpu.SemaphoreType.DMA(()))
    args = (group, packed)
    own, *parts, active, slope, narrow = call(
        body, outs, args, 1000000, 1000000, far=(1,), scratch=scratch, name="feed_one"
    )
    return own, return_parts(parts), active, slope, narrow


def feed_backward(place, group, active, slope, narrow, packed):
    def body(
        place, group, active, slope, narrow, far, own, part_a, part_b, part_c, grad_out, sent, near, sem
    ):
        copy = pltpu.make_async_copy(far.at[:, PACKED : PACKED + D], near, sem)
        copy.start()
        other = pl.ds(pl.multiple_of((1 - place[1]) * 512, 128), 512)
        sent[:, 512:1024] = active[:, other]
        for low in range(0, 512, 256):
            rows = slice(low, low + 256)
            grad = dot_nt(group[rows, :], narrow[...]) * slope[rows, :].astype(f32)
            grad = grad.astype(bf16)
            grad_out[rows, :] = grad
            if low == 0:
                copy.wait()
            terms = dot_nt(grad, near[...])
            first, second = ((own, part_a), (part_b, part_c))[low // 256]
            first[...] = terms[0:ROWS].astype(first.dtype)
            second[...] = terms[ROWS : 2 * ROWS].astype(bf16)
        sent[:, 0:512] = grad_out[:, other]

    outs = (
        shape(ROWS, D, dtype=f32),
        shape(ROWS, D),
        shape(ROWS, D),
        shape(ROWS, D),
        shape(512, D),
        shape(512, D),
    )
    scratch = (pltpu.VMEM((D, D), bf16), pltpu.SemaphoreType.DMA(()))
    args = (place, group, active, slope, narrow, packed)
    own, *parts, grad, sent = call(
        body, outs, args, 1000000, 1000000, far=(5,), scratch=scratch, name="feed_one_back"
    )
    return own, return_parts(parts), grad, sent


def gelu_pieces(x):
    k = 0.7978845608028654
    square = x * x
    bend = jnp.tanh(k * (x + 0.044715 * (square * x)))
    half = 0.5 * (1.0 + bend)
    slope = half + x * (0.5 * (1.0 - bend * bend)) * (k * (1.0 + 3 * 0.044715 * square))
    return x * half, slope


def grid_call(body, grid, in_specs, outs, out_specs, scratch, args, flops, moved, name):
    return pl.pallas_call(
        body,
        grid=grid,
        in_specs=in_specs,
        out_shape=outs,
        out_specs=out_specs,
        scratch_shapes=scratch,
        compiler_params=pltpu.CompilerParams(
            vmem_limit_bytes=LIMIT, dimension_semantics=("arbitrary",)
        ),
        cost_estimate=pl.CostEstimate(flops=flops, bytes_accessed=moved, transcendentals=0),
        name=name,
    )(*args)


def fixed(rows, columns):
    return pl.BlockSpec(
        (rows, columns), lambda i: (0, 0), pipeline_mode=pl.Buffered(buffer_count=1)
    )


def rows_of(rows, columns):
    return pl.BlockSpec((rows, columns), lambda i: (i, 0))


def owner_forward(rows, expander, reducer):
    def body(rows, expander, reducer, active_out, slope_out, parts_out):
        active, slope = gelu_pieces(dot(rows[...], expander[...]))
        active = active.astype(bf16)
        active_out[...] = active
        slope_out[...] = slope.astype(bf16)
        parts_out[...] = dot(active, reducer[...]).astype(bf16)

    block = rows_of(512, D)
    return grid_call(
        body,
        (2,),
        [block, fixed(D, D), fixed(D, D)],
        (shape(1024, D),) * 3,
        [block] * 3,
        [],
        (rows, expander, reducer),
        4300000000,
        12000000,
        "owner",
    )


def owner_backward(incoming, slope, expander, reducer):
    def body(incoming, slope, expander, reducer, grad_out, rows_out):
        grad = (dot_nt(incoming[...], reducer[...]) * slope[...].astype(f32)).astype(bf16)
        grad_out[...] = grad
        rows_out[...] = dot_nt(grad, expander[...]).astype(bf16)

    block = rows_of(256, D)
    return grid_call(
        body,
        (4,),
        [block, block, fixed(D, D), fixed(D, D)],
        (shape(1024, D),) * 2,
        [block] * 2,
        [],
        (incoming, slope, expander, reducer),
        4300000000,
        12000000,
        "owner_back",
    )


def places(kind):
    row = lax.broadcasted_iota(jnp.int32, (128, 256), 0)
    column = lax.broadcasted_iota(jnp.int32, (128, 256), 1)
    return (column == (row // 4) * 8 + kind * 4 + row % 4).astype(bf16)


def owner_both(arrived, expander, reducer):
    def body(arrived, expander, reducer, rows, grads, active_out, grad_out, sent):
        for block in range(2):
            packed = arrived[block * 256 : (block + 1) * 256, :]
            place = slice(block * 128, (block + 1) * 128)
            rows[place, :] = dot(places(0), packed).astype(bf16)
            grads[place, :] = dot(places(1), packed).astype(bf16)
        for low in range(0, 2048, 512):
            units = slice(low, low + 512)
            active, slope = gelu_pieces(dot(rows[...], expander[:, units]))
            active_out[:, units] = active.astype(bf16)
            grad_out[:, units] = (dot_nt(grads[...], reducer[units, :]) * slope).astype(bf16)
        parts = dot(active_out[...], reducer[...]).astype(bf16)
        returned = dot_nt(grad_out[...], expander[...]).astype(bf16)
        for block in range(2):
            place = slice(block * 128, (block + 1) * 128)
            sent[block * 256 : (block + 1) * 256, :] = (
                dot_tn(places(0), parts[place]) + dot_tn(places(1), returned[place])
            ).astype(bf16)

    return grid_call(
        body,
        (2,),
        [rows_of(512, D), fixed(D, 2048), fixed(2048, D)],
        (shape(512, D), shape(512, D), shape(512, 2048), shape(512, 2048), shape(1024, D)),
        [rows_of(256, D), rows_of(256, D), rows_of(256, 2048), rows_of(256, 2048), rows_of(512, D)],
        [],
        (arrived, expander, reducer),
        9000000000,
        20000000,
        "owner_both",
    )


def feed_both(place, mine, partner, weights):
    def body(place, mine, partner, far, own, other, active, grad, sent, rows, near, sems):
        copies = []
        for i, low in enumerate((0, 2 * D, D, 3 * D)):
            copy = pltpu.make_async_copy(
                far.at[:, low : low + D], near.at[:, low : low + D], sems.at[i]
            )
            copy.start()
            copies.append(copy)
        rows[0:ROWS, :] = mine[...]
        rows[ROWS : 2 * ROWS, :] = partner[...]
        for part in range(2):
            units = slice(part * D, part * D + D)
            narrow = slice(2 * D + part * D, 3 * D + part * D)
            copies[2 * part].wait()
            value, slope = gelu_pieces(dot(rows[:, 0:D], near[:, units]))
            active[:, units] = value.astype(bf16)
            copies[2 * part + 1].wait()
            back = dot_nt(rows[:, D : 2 * D], near[:, narrow]) * slope
            grad[:, units] = back.astype(bf16)
        dense = dot(active[:, 0:D], near[:, 2 * D : 3 * D]) + dot(
            active[:, D : 2 * D], near[:, 3 * D : 4 * D]
        )
        own[:, 0:D] = dense[0:ROWS]
        other[:, 0:D] = dense[ROWS : 2 * ROWS].astype(bf16)
        back = dot_nt(grad[...], near[:, 0 : 2 * D])
        own[:, D : 2 * D] = back[0:ROWS]
        other[:, D : 2 * D] = back[ROWS : 2 * ROWS].astype(bf16)
        twin = pl.ds(pl.multiple_of((1 - place[1]) * D, 128), D)
        sent[:, 0:D] = active[:, twin]
        sent[:, D : 2 * D] = grad[:, twin]

    outs = (
        shape(ROWS, 2 * D, dtype=f32),
        shape(ROWS, 2 * D),
        shape(2 * ROWS, 2 * D),
        shape(2 * ROWS, 2 * D),
        shape(2 * ROWS, 2 * D),
    )
    scratch = (
        pltpu.VMEM((2 * ROWS, 2 * D), bf16),
        pltpu.VMEM((D, 4 * D), bf16),
        pltpu.SemaphoreType.DMA((4,)),
    )
    args = (place, mine, partner, weights)
    return call(body, outs, args, 1000000, 1000000, far=(3,), scratch=scratch, name="feed")


def feed_gradients(place, mine, partner, twins, active, grad, got):
    def body(place, mine, partner, twins, active, grad, got, out):
        base = place[1] * D

        for low in range(0, D, 256):
            column = slice(low, low + 256)
            units = pl.ds(pl.multiple_of(base + low, 128), 256)
            normed = slice(low, low + 256)
            values = grad[:, pl.ds(pl.multiple_of(base, 128), D)]
            out[column, 0:D] = (
                dot_tn(mine[:, normed], values[0:ROWS])
                + dot_tn(partner[:, normed], values[ROWS : 2 * ROWS])
                + dot_tn(twins[:, normed], got[:, D : 2 * D])
            ).astype(bf16)
            out[column, D : 2 * D] = (
                dot_tn(active[0:ROWS, units], mine[:, D : 2 * D])
                + dot_tn(active[ROWS : 2 * ROWS, units], partner[:, D : 2 * D])
                + dot_tn(got[:, column], twins[:, D : 2 * D])
            ).astype(bf16)

    args = (place, mine, partner, twins, active, grad, got)
    outs = (shape(D, 4224),)
    return pl.pallas_call(
        body,
        grid=(1,),
        in_specs=[pl.BlockSpec(memory_space=pltpu.SMEM)]
        + [pl.BlockSpec(arg.shape, lambda i: (0, 0)) for arg in args[1:]],
        out_shape=outs,
        out_specs=[pl.BlockSpec((D, 2 * D), lambda i: (0, 0))],
        compiler_params=pltpu.CompilerParams(vmem_limit_bytes=LIMIT),
        cost_estimate=pl.CostEstimate(flops=1000000, bytes_accessed=1000000, transcendentals=0),
        name="feed_gradients",
    )(*args)[0]


def after(value, *others):
    return lax.optimization_barrier((value, *others))[0]


def gather_line(value):
    return jnp.concatenate(around(value), axis=0)


def return_parts(parts):
    return shift(parts[0], "z", -1), shift(parts[1], "z", 1), shift(parts[2], "z", 2)


def around(value):
    return value, shift(value, "z", 1), shift(value, "z", -1), shift(value, "z", 2)


def positions(route):
    chosen = route[:, 0]
    row = jnp.arange(ROWS, dtype=jnp.int32)
    earlier = (row[None, :] < row[:, None]) & (row[None, :] // SEQ == row[:, None] // SEQ)
    same = (chosen[None, :] == chosen[:, None]) & earlier
    return chosen, row // SEQ, jnp.sum(same.astype(jnp.int32), axis=1)


def slots_first(route):
    chosen, sequence, position = positions(route)
    slot = chosen * 8 + sequence * 4 + position
    return slot[:, None], slot[None, :]


def slots_second(route):
    chosen, sequence, position = positions(route)
    slot = (chosen // 32) * 256 + (chosen % 32) * 8 + sequence * 2 + position
    return slot[:, None], slot[None, :]


def exchange(rows):
    blocks = rows.reshape(128, 8, rows.shape[-1])
    moved = lax.all_to_all(blocks, ALL, split_axis=0, concat_axis=0, tiled=True)
    return moved.reshape(rows.shape)


def exchange_plane(packed):
    blocks = packed.reshape(16, 64, packed.shape[1])
    return lax.all_to_all(blocks, PLANE, split_axis=0, concat_axis=0, tiled=True)


def few_rows(few):
    pick = lax.broadcasted_iota(jnp.int32, (8, 128), 0) == lax.broadcasted_iota(
        jnp.int32, (8, 128), 1
    )
    return lax.dot_general(
        pick.astype(f32),
        few,
        (((1,), (1,)), ((), ())),
        precision=lax.Precision.HIGHEST,
        preferred_element_type=f32,
    )


def write_few(total, mixer, gain, regain):
    rows = few_rows(total)
    mixer[...] = rows[0:2]
    gain[...] = rows[2:3]
    regain[...] = rows[3:4]


FEW = (
    jax.ShapeDtypeStruct((2, 32), f32),
    jax.ShapeDtypeStruct((1, 32), f32),
    jax.ShapeDtypeStruct((1, 32), f32),
)


def add_blocks(blocks):
    return jnp.sum(blocks.astype(f32), axis=0).astype(bf16)


def pack_attention(inner, outer, mixer, gain, regain):
    blank = jnp.zeros((inner.shape[0], 124), bf16)
    return jnp.concatenate([inner, outer, mixer, gain[:, None], regain[:, None], blank], axis=1)


def pack_feed_first(widen, narrow):
    z = lax.axis_index("z")
    units = widen.reshape(32, 16, 2, 4, 32)
    units = lax.dynamic_index_in_dim(units, z, 3, keepdims=False)
    columns = units.transpose(0, 2, 1, 3).reshape(32, 1024)
    return jnp.concatenate([columns, lax.dynamic_slice_in_dim(narrow, z * 32, 32, 0)], axis=1)


def pack_feed_second(widen, narrow):
    half = lax.rem(lax.axis_index("z"), 2)
    units = widen.reshape(32, 16, 2, 2, 2, 32)
    units = lax.dynamic_index_in_dim(units, half, 3, keepdims=False)
    columns = units.transpose(0, 3, 1, 2, 4).reshape(32, 2048)
    rows = half_of(narrow, half, 0)
    return jnp.concatenate([columns, rows[:32], rows[32:]], axis=1)


def quarter(place, i):
    return lax.rem(place[0] + (0, 3, 1, 2)[i], 4)


def finish_second(place, summed):
    c = lax.axis_index("c")
    got = swap(lax.dynamic_slice_in_dim(summed, 32 * (1 - c), 32, 1))

    def body(place, summed, got, widen, narrow, inner, outer, mixer, gain, regain):
        lane = lax.broadcasted_iota(jnp.int32, (32, 128), 1) // 32
        rows = pl.ds(pl.multiple_of(place[1] * 32, 32), 32)

        def mine(z, low, size):
            return summed[z, rows, low : low + size].astype(f32)

        def twin(z, low, size):
            return got[z, :, low : low + size].astype(f32)

        for index, (core, term) in enumerate(((place[1], mine), (1 - place[1], twin))):
            for low in range(0, 1024, 128):
                for half in range(2):
                    value = term(half, low, 128) + term(half + 2, low, 128)
                    target = half * 2 + core
                    for k in range(4):
                        moved = pltpu.roll(value, lax.rem(target * 32 + (128 - k * 32), 128), 1)
                        column = (low // 32 + k) * 128
                        out = widen.at[:, column : column + 128]
                        if index == 0 and half == 0:
                            out[...] = moved
                        else:
                            out[...] = jnp.where(lane == target, moved, out[...])
            for half in range(2):
                place_in = pl.multiple_of(half * 64 + core * 32, 32)
                narrow[pl.ds(place_in, 32), :] = term(half, 1024, 1024) + term(half + 2, 1024, 1024)
            for out, low, size in ((inner, 2048, 1536), (outer, 3584, 512)):
                total = (term(0, low, size) + term(1, low, size)) + (
                    term(2, low, size) + term(3, low, size)
                )
                out[:, pl.ds(pl.multiple_of(core * size, 128), size)] = total
        total = jnp.zeros((32, 128), f32)
        for z in range(4):
            total += mine(z, 4096, 128) + twin(z, 4096, 128)
        write_few(total, mixer, gain, regain)

    outs = (
        shape(32, 4096, dtype=f32),
        shape(ROWS, D, dtype=f32),
        shape(32, 3072, dtype=f32),
        shape(32, D, dtype=f32),
        *FEW,
    )
    widen, narrow, inner, outer, mixer, gain, regain = call(
        body, outs, (place, summed, got), 1000000, 1000000, name="second_out"
    )
    return (widen, narrow), (inner, outer), (mixer.T, gain.reshape(32), regain.reshape(32))


def finish_feed_first(place, blocks):
    c = lax.axis_index("c")
    summed = add_blocks(blocks)
    widen = summed[:, :512]
    widen = in_order(c, half_of(widen, c, 0), swap(half_of(widen, 1 - c, 0)), 1)
    narrow = jnp.concatenate([summed[:32, 512:], summed[32:, 512:]], axis=1)
    pieces = around(jnp.concatenate([widen, narrow], axis=0))

    def body(place, own, before, later, opposite, widen, narrow):
        lane = lax.broadcasted_iota(jnp.int32, (32, 128), 1) // 32
        for i, source in enumerate((own, before, later, opposite)):
            z = quarter(place, i)
            narrow[pl.ds(pl.multiple_of(z * 32, 32), 32), :] = source[32:64, :].astype(f32)
            for core in range(2):
                for four in range(4):
                    column = core * 512 + four * 128
                    value = source[0:32, column : column + 128].astype(f32)
                    for k in range(4):
                        moved = pltpu.roll(value, lax.rem(z * 32 + (128 - k * 32), 128), 1)
                        low = (four * 4 + k) * 256 + core * 128
                        out = widen.at[:, low : low + 128]
                        if i == 0:
                            out[...] = moved
                        else:
                            out[...] = jnp.where(lane == z, moved, out[...])

    outs = (shape(32, 4096, dtype=f32), shape(ROWS, D, dtype=f32))
    return call(body, outs, (place, *pieces), 1000000, 1000000, name="feed_one_out")


def finish_attention_first(place, blocks, earlier):
    summed = jnp.sum(blocks.reshape(16, 2, 32, 640).astype(f32), axis=0).astype(bf16)
    pieces = lax.optimization_barrier((*around(summed), earlier))[:4]

    def body(place, own, before, later, opposite, inner, outer, mixer, gain, regain):
        sources = (own, before, later, opposite)
        halves = []
        for core in range(2):
            one, two, three, four = (x[core, :, 512:640].astype(f32) for x in sources)
            halves.append((one + four) + (two + three))
        write_few(halves[0] + halves[1], mixer, gain, regain)
        for i, source in enumerate(sources):
            z = quarter(place, i)
            for core in range(2):
                index = z * 2 + core
                inner[:, pl.ds(pl.multiple_of(index * 384, 128), 384)] = source[
                    core, :, 0:384
                ].astype(f32)
                outer[:, pl.ds(pl.multiple_of(index * 128, 128), 128)] = source[
                    core, :, 384:512
                ].astype(f32)

    outs = (shape(32, 3072, dtype=f32), shape(32, D, dtype=f32), *FEW)
    inner, outer, mixer, gain, regain = call(
        body, outs, (place, *pieces), 1000000, 1000000, name="attention_out"
    )
    return inner, outer, mixer.T, gain.reshape(32), regain.reshape(32)


def on_device(
    tokens,
    cotangent,
    routes_first,
    routes_second,
    inner_first,
    outer_first,
    widen_first,
    narrow_first,
    mixer_first,
    gain_first,
    regain_first,
    inner_second,
    outer_second,
    widen_second,
    narrow_second,
    mixer_second,
    gain_second,
    regain_second,
    expand_first,
    reduce_first,
    expand_second,
    reduce_second,
):
    place = jnp.stack([lax.axis_index("z"), lax.axis_index("c")]).astype(jnp.int32)
    gathered_first = lax.all_gather(
        jnp.concatenate(
            [
                pack_attention(inner_first, outer_first, mixer_first, gain_first, regain_first),
                pack_feed_first(widen_first, narrow_first),
            ],
            axis=1,
        ),
        ("x", "y", "c"),
        axis=0,
        tiled=True,
    )
    gathered_second = lax.all_gather(
        pack_attention(inner_second, outer_second, mixer_second, gain_second, regain_second),
        ("x", "y", "c"),
        axis=0,
        tiled=True,
    )
    gathered_feed = lax.all_gather(
        pack_feed_second(widen_second, narrow_second), ("x", "y", "c"), axis=0, tiled=True
    )
    column_first, row_first = slots_first(routes_first)
    column_second, row_second = slots_second(routes_second)
    expander, reducer = expand_first[0], reduce_first[0]

    pair, joint, middle, normed_two, shares, send = first_front(tokens, gathered_first, row_first)
    received = exchange(send)
    group = gather_line(normed_two)
    received = after(received, group)
    active, slope, parts = owner_forward(received, expander, reducer)
    back = exchange(parts)
    dense_own, dense_parts, active_feed, slope_feed, narrow_one = feed_forward(
        after(group, parts), gathered_first
    )

    output, stream, dense, expert, pair_s, joint_s, middle_s, feed_s, shares_s, send = second_front(
        back,
        column_first,
        middle,
        shares,
        dense_own,
        dense_parts,
        cotangent,
        gathered_second,
        row_second,
    )
    arrived = exchange(send)
    feed_flipped = flip(feed_s)
    arrived = after(arrived, feed_flipped)
    line = lax.all_gather(after(pair, arrived), COLUMN, axis=0, tiled=True)
    rows, incoming_s, active_s, grad_s, sent = owner_both(
        arrived, expand_second[0], reduce_second[0]
    )
    back = exchange(sent)
    terms, terms_partner, active_second, grad_second, feed_sent = feed_both(
        place, feed_s, after(feed_flipped, sent), gathered_feed
    )
    flipped = flip(terms_partner)
    feed_gradient = feed_gradients(
        place,
        feed_s,
        feed_flipped,
        swap(jnp.concatenate([feed_s, feed_flipped], axis=0)),
        active_second,
        grad_second,
        swap(feed_sent),
    )
    back = after(back, feed_gradient)
    pair_twin = swap(pair_s)
    back = after(back, line, pair_twin)
    output_two, upstream, mine, other, small, grad_dense, send = second_back(
        place,
        back,
        column_second,
        cotangent,
        middle_s,
        shares_s,
        terms,
        flipped,
        feed_s,
        joint_s,
        stream,
        gathered_second,
        shares,
        row_first,
    )
    grad_s = after(grad_s, send)
    grad_expand_two = dot_tn(rows, grad_s)
    grad_reduce_two = dot_tn(active_s, after(incoming_s, send))

    grad_group = gather_line(grad_dense)
    incoming = after(exchange(send), grad_expand_two, grad_reduce_two, grad_group)
    grad_first, grad_rows = owner_backward(incoming, slope, expander, reducer)
    feed_own, feed_parts, grad_hidden, feed_sent = feed_backward(
        place,
        after(grad_group, grad_rows),
        active_feed,
        slope_feed,
        narrow_one,
        gathered_first,
    )
    packed = weights_second(feed_gradient, pair_s, pair_twin, mine, swap(other), small)
    packed = lax.psum_scatter(packed, PLANE, scatter_dimension=0, tiled=True)
    back = exchange(grad_rows)
    feed_packed = weights_feed(
        place,
        group,
        swap(group),
        grad_hidden,
        active_feed,
        swap(feed_sent),
        grad_group,
        swap(grad_group),
    )
    grad_expand_one = dot_tn(received, grad_first)
    grad_reduce_one = dot_tn(active, incoming)
    back = after(back, grad_expand_one, grad_reduce_one, *feed_parts)
    back = after(back, feed_packed)
    feed_sums = exchange_plane(after(feed_packed, back))
    gradient_tokens, mine, other, small = first_back(
        place,
        back,
        column_first,
        upstream,
        middle,
        shares,
        dense,
        expert,
        feed_own,
        feed_parts,
        normed_two,
        joint,
        tokens,
        gathered_first,
    )
    got = swap(other)
    ahead = [jnp.concatenate([mine[i], got[i]], axis=0) for i in (1, 2, 3)]
    parts = (shift(ahead[0], "z", 1), shift(ahead[1], "z", -1), shift(ahead[2], "z", 2))
    first_packed = weights_first(place, line, mine, got, parts, small)
    first_packed = after(first_packed, feed_sums)
    packed = lax.all_gather(after(packed, first_packed), "z", axis=0)
    blocks = lax.all_to_all(
        first_packed.reshape(32, 32, 640), ("x", "y", "c"), split_axis=0, concat_axis=0, tiled=True
    )
    feed_finals = finish_feed_first(place, feed_sums)
    packed = after(packed, feed_finals)
    feed_finals_second, finals_second, few_second = finish_second(place, packed)
    inner, outer, *few_first = finish_attention_first(
        place, blocks, (feed_finals, feed_finals_second, finals_second)
    )
    return (
        (output, output_two, gradient_tokens)
        + (inner, outer)
        + tuple(feed_finals)
        + tuple(few_first)
        + finals_second
        + tuple(feed_finals_second)
        + few_second
        + (
            grad_expand_one[None],
            grad_reduce_one[None],
            grad_expand_two[None],
            grad_reduce_two[None],
        )
    )


def solution(mesh):
    fine = Mesh(mesh.devices.reshape(4, 4, 4, 2), ALL)
    owner = ("x", "y", "c")
    tokens = P(ALL, None)
    dense = (P(owner, None),) * 5 + (P(owner),) * 2
    experts = (
        P(owner, None, "z"),
        P(owner, "z", None),
        P(ALL, None, None),
        P(ALL, None, None),
    )
    return jax.shard_map(
        on_device,
        mesh=fine,
        in_specs=(tokens,) * 4 + dense + dense + experts,
        out_specs=(tokens,) * 3 + dense + dense + experts,
        check_vma=False,
    )
```

```python
import jax
import jax.numpy as jnp
from jax import lax
from jax.experimental import pallas as pl
from jax.experimental.pallas import tpu as pltpu
from jax.sharding import Mesh, PartitionSpec as P

HEADS = 16
HEAD = 64
SEQ = 64
ROWS = 128
D = 1024
PACKED = 4224
SCALE = HEAD**-0.5
ALL = ("z", "x", "y", "c")
PLANE = ("x", "y")
COLUMN = ("z", "c")
SIZES = {"z": 4, "x": 4, "y": 4, "c": 2}
epsilon = 1e-05
bf16 = jnp.bfloat16
f32 = jnp.float32
LIMIT = 52 * 1024 * 1024


def shift(value, axis, step):
    size = SIZES[axis]
    return lax.ppermute(value, axis, [(i, (i + step) % size) for i in range(size)])


def swap(value):
    return shift(value, "c", 1)


def flip(value):
    return lax.ppermute(value, "z", [(0, 1), (1, 0), (2, 3), (3, 2)])


def dot(a, b):
    return jnp.dot(a, b, preferred_element_type=f32)


def dot_tn(a, b):
    return lax.dot_general(a, b, (((0,), (0,)), ((), ())), preferred_element_type=f32)


def dot_nt(a, b):
    return lax.dot_general(a, b, (((1,), (1,)), ((), ())), preferred_element_type=f32)


def in_order(core, mine, twin, axis):
    return jnp.where(
        core == 0,
        jnp.concatenate([mine, twin], axis=axis),
        jnp.concatenate([twin, mine], axis=axis),
    )


def half_of(value, which, axis):
    size = value.shape[axis] // 2
    return lax.dynamic_slice_in_dim(value, which * size, size, axis)


def shape(*dims, dtype=bf16):
    return jax.ShapeDtypeStruct(dims, dtype)


def whole():
    return pl.BlockSpec(memory_space=pltpu.VMEM)


def space_of(value):
    if value.dtype == jnp.int32 and value.ndim == 1:
        return pl.BlockSpec(memory_space=pltpu.SMEM)
    return whole()


def call(body, outs, args, flops, moved, far=(), scratch=(), name=None):
    return pl.pallas_call(
        body,
        out_shape=outs,
        in_specs=[
            pl.BlockSpec(memory_space=pl.ANY) if i in far else space_of(arg)
            for i, arg in enumerate(args)
        ],
        out_specs=[whole()] * len(outs),
        scratch_shapes=list(scratch),
        compiler_params=pltpu.CompilerParams(vmem_limit_bytes=LIMIT),
        cost_estimate=pl.CostEstimate(flops=flops, bytes_accessed=moved, transcendentals=0),
        name=name,
    )(*args)


def start_weights(far, near, sems):
    copies = []
    for i, low, high in ((4, 4096, 4224), (0, 0, D), (1, D, 2 * D), (2, 2 * D, 3 * D), (3, 3 * D, 4096)):
        copy = pltpu.make_async_copy(
            far.at[:, low:high], near.at[:, low:high], sems.at[i]
        )
        copy.start()
        copies.append(copy)
    return copies


WEIGHTS = (pltpu.VMEM((D, PACKED), bf16), pltpu.SemaphoreType.DMA((5,)))


def vector_rows(near):
    pick = lax.broadcasted_iota(jnp.int32, (8, 128), 0) == lax.broadcasted_iota(
        jnp.int32, (8, 128), 1
    )
    return dot_nt(pick.astype(bf16), near[:, 4096:4224])


def normalize(values):
    center = values - jnp.mean(values, axis=-1, keepdims=True)
    spread = jnp.mean(center * center, axis=-1, keepdims=True)
    inverse = lax.rsqrt(spread + epsilon)
    return center * inverse, inverse


def normalize_backward(hat, inverse, gradient):
    return inverse * (
        gradient
        - jnp.mean(gradient, axis=-1, keepdims=True)
        - hat * jnp.mean(gradient * hat, axis=-1, keepdims=True)
    )


def lane_half(rows=ROWS):
    return lax.broadcasted_iota(jnp.int32, (rows, 128), 1) < HEAD


def split_heads(pair):
    first = lane_half()
    blank = jnp.zeros_like(pair)
    return jnp.concatenate([jnp.where(first, pair, blank), jnp.where(first, blank, pair)], axis=0)


def own_sequence(table):
    first = lane_half(SEQ)
    return [
        jnp.where(first, table[low : low + SEQ], table[low + SEQ : low + 2 * SEQ])
        for low in (0, ROWS)
    ]


def spread_sequences(blocks):
    first = lane_half(SEQ)
    parts = []
    for block in blocks:
        parts += [jnp.where(first, block, 0.0), jnp.where(first, 0.0, block)]
    return jnp.concatenate(parts, axis=0).astype(bf16)


def attention_of(query, keys):
    key = lax.broadcasted_iota(jnp.int32, (SEQ, ROWS), 0)
    place = jnp.bitwise_and(lax.broadcasted_iota(jnp.int32, (SEQ, ROWS), 1), SEQ - 1)
    result = []
    for scores in own_sequence(dot_nt(split_heads(keys), query) * SCALE):
        scores = jnp.where(key <= place, scores, -1e30)
        raised = jnp.exp(scores - jnp.max(scores, axis=0, keepdims=True))
        result.append(raised / jnp.sum(raised, axis=0, keepdims=True))
    return result


def pair_of(ref, part, pair):
    return ref[:, pl.ds(pl.multiple_of(part * D + pair * 128, 128), 128)]


def front(stream, near, copies, normed_out, joint_out, mixed_out, middle_out, two_out, share_out):
    copies[0].wait()
    vectors = vector_rows(near)
    hat, _ = normalize(stream)
    normed = (hat * vectors[2:3]).astype(bf16)
    normed_out[...] = normed
    for part in range(3):
        copies[part + 1].wait()
        for low in range(part * D, part * D + D, 512):
            joint_out[:, low : low + 512] = dot(normed, near[:, low : low + 512]).astype(bf16)

    @pl.loop(0, HEADS // 2, unroll=True)
    def _(pair):
        query, keys, values = (pair_of(joint_out, part, pair) for part in range(3))
        table = spread_sequences(attention_of(query, keys))
        one = dot_tn(table[0:ROWS], values)
        two = dot_tn(table[ROWS : 2 * ROWS], values)
        column = pl.ds(pl.multiple_of(pair * 128, 128), 128)
        mixed_out[:, column] = jnp.where(lane_half(), one, two).astype(bf16)

    mixed = mixed_out[...]
    copies[4].wait()
    for low in range(0, D, 512):
        middle_out[:, low : low + 512] = stream[:, low : low + 512] + dot(
            mixed, near[:, 3072 + low : 3072 + low + 512]
        )
    hat, _ = normalize(middle_out[...])
    normed_two = (hat * vectors[3:4]).astype(bf16)
    two_out[...] = normed_two
    logits = dot(normed_two, near[:, 4096:4224])
    one, two = logits[:, 0:1], logits[:, 1:2]
    top = jnp.maximum(one, two)
    one, two = jnp.exp(one - top), jnp.exp(two - top)
    total = one + two
    one, two = one / total, two / total
    lane = lax.broadcasted_iota(jnp.int32, (ROWS, 128), 1)
    share_out[...] = jnp.where(lane == 0, one, two)
    return normed_two, one, two


def send_first(rows, slot_row, out):
    slots = lax.broadcasted_iota(jnp.int32, (256, ROWS), 0)
    table = (slots == slot_row[...]).astype(bf16)
    buffer = dot(table, rows).astype(bf16)
    for z in range(4):
        out[z * 256 : (z + 1) * 256, :] = buffer


def send_second(rows, grads, slot_row, out):
    slots = lax.broadcasted_iota(jnp.int32, (256, ROWS), 0)
    for group in range(2):
        wanted = slot_row[...] - group * 256
        buffer = dot((slots == wanted).astype(bf16), rows) + dot(
            (slots == wanted + 4).astype(bf16), grads
        )
        buffer = buffer.astype(bf16)
        for z in (2 * group, 2 * group + 1):
            out[z * 256 : (z + 1) * 256, :] = buffer


def take_first(back, slot_column):
    column = lax.broadcasted_iota(jnp.int32, (ROWS, 1024), 1)
    table = (slot_column[...] == jnp.bitwise_and(column, 255)).astype(bf16)
    return dot(table, back[...])


def take_second(back, slot_column):
    column = lax.broadcasted_iota(jnp.int32, (ROWS, 1024), 1)
    place = jnp.where(column >= 512, 256, 0) + jnp.bitwise_and(column, 255)
    rows = dot((slot_column[...] == place).astype(bf16), back[...])
    grads = dot((slot_column[...] + 4 == place).astype(bf16), back[...])
    return rows, grads


def backward(
    stream,
    near,
    copies,
    joint_ref,
    middle,
    normed_two,
    one,
    two,
    upstream,
    dense,
    expert,
    incoming,
    joint_out,
    attended_out,
    small_out,
    mixed_ref,
):
    copies[0].wait()
    vectors = vector_rows(near)
    first = jnp.sum(upstream * dense, axis=1, keepdims=True)
    second = jnp.sum(upstream * expert, axis=1, keepdims=True)
    both = one * first + two * second
    first, second = one * (first - both), two * (second - both)
    normed_two = normed_two.astype(f32)
    gradient = first * vectors[0:1] + second * vectors[1:2] + incoming
    hat, inverse = normalize(middle)
    small_out[0:1, :] = jnp.sum(normed_two * first, axis=0, keepdims=True)
    small_out[1:2, :] = jnp.sum(normed_two * second, axis=0, keepdims=True)
    small_out[3:4, :] = jnp.sum(gradient * hat, axis=0, keepdims=True)
    small_out[4:8, :] = jnp.zeros((4, D), f32)
    grad_middle = upstream + normalize_backward(hat, inverse, gradient * vectors[3:4])
    attended = grad_middle.astype(bf16)
    attended_out[...] = attended
    copies[4].wait()
    for low in range(0, D, 512):
        mixed_ref[:, low : low + 512] = dot_nt(attended, near[low : low + 512, 3072:4096]).astype(
            bf16
        )

    @pl.loop(0, HEADS // 2, unroll=True)
    def _(pair):
        query, keys, values = (pair_of(joint_ref, part, pair) for part in range(3))
        column = pl.ds(pl.multiple_of(pair * 128, 128), 128)
        grad_mixed = mixed_ref[:, column]
        attention = attention_of(query, keys)
        grad_attention = own_sequence(dot_nt(split_heads(values), grad_mixed))
        grad_scores = [
            weight * (grad - jnp.sum(weight * grad, axis=0, keepdims=True))
            for weight, grad in zip(attention, grad_attention)
        ]
        grad_scores = spread_sequences(grad_scores)
        grad_keys = dot(grad_scores, query) * SCALE
        grad_values = dot(spread_sequences(attention), grad_mixed)
        halves = (
            (
                dot_tn(grad_scores[0:ROWS], keys) * SCALE,
                dot_tn(grad_scores[ROWS : 2 * ROWS], keys) * SCALE,
            ),
            (grad_keys[0:ROWS], grad_keys[ROWS : 2 * ROWS]),
            (grad_values[0:ROWS], grad_values[ROWS : 2 * ROWS]),
        )
        for part in range(3):
            place = pl.ds(pl.multiple_of(part * D + pair * 128, 128), 128)
            joint_out[:, place] = jnp.where(lane_half(), *halves[part]).astype(bf16)

    for copy in copies[1:4]:
        copy.wait()
    parts = []
    for low in range(0, D, 256):
        parts.append(dot_nt(joint_out[...], near[low : low + 256, 0:3072]))
    grad_normed = jnp.concatenate(parts, axis=1)
    hat, inverse = normalize(stream)
    small_out[2:3, :] = jnp.sum(grad_normed * hat, axis=0, keepdims=True)
    return grad_middle + normalize_backward(hat, inverse, grad_normed * vectors[2:3])


def halves_of(pair):
    return pair.at[:, 0:D], pair.at[:, D : 2 * D]


def first_front(tokens, weights, slot_row):
    def body(tokens, far, slot_row, pair, joint, middle, two, shares, send, near, sems):
        copies = start_weights(far, near, sems)
        normed, mixed = halves_of(pair)
        rows, _, _ = front(
            tokens[...].astype(f32), near, copies, normed, joint, mixed, middle, two, shares
        )
        send_first(rows, slot_row, send)

    outs = (
        shape(ROWS, 2 * D),
        shape(ROWS, 3 * D),
        shape(ROWS, D, dtype=f32),
        shape(ROWS, D),
        shape(ROWS, 128, dtype=f32),
        shape(1024, D),
    )
    args = (tokens, weights, slot_row)
    return call(body, outs, args, 1300000000, 14000000, far=(1,), scratch=WEIGHTS, name="front")


def second_front(back, slot_column, middle, shares, own, parts, cotangent, weights, slot_row):
    def body(
        back,
        slot_column,
        middle,
        shares,
        own,
        part_a,
        part_b,
        part_c,
        cotangent,
        far,
        slot_row,
        low_out,
        stream_out,
        dense_out,
        expert_out,
        pair,
        joint,
        middle_out,
        feed,
        shares_out,
        send,
        near,
        sems,
    ):
        copies = start_weights(far, near, sems)
        expert = take_first(back, slot_column)
        dense = own[...] + part_a[...].astype(f32) + part_b[...].astype(f32) + part_c[...].astype(f32)
        dense_out[...] = dense
        expert_out[...] = expert
        stream = middle[...] + shares[:, 0:1] * dense + shares[:, 1:2] * expert
        stream_out[...] = stream
        low_out[...] = stream.astype(bf16)
        normed, mixed = halves_of(pair)
        two, grad_dense = halves_of(feed)
        rows, one, other = front(
            stream, near, copies, normed, joint, mixed, middle_out, two, shares_out
        )
        upstream = cotangent[...].astype(f32)
        grad_dense[...] = (upstream * one).astype(bf16)
        send_second(rows, (upstream * other).astype(bf16), slot_row, send)

    outs = (
        shape(ROWS, D),
        shape(ROWS, D, dtype=f32),
        shape(ROWS, D, dtype=f32),
        shape(ROWS, D, dtype=f32),
        shape(ROWS, 2 * D),
        shape(ROWS, 3 * D),
        shape(ROWS, D, dtype=f32),
        shape(ROWS, 2 * D),
        shape(ROWS, 128, dtype=f32),
        shape(1024, D),
    )
    args = (back, slot_column, middle, shares, own, *parts, cotangent, weights, slot_row)
    return call(body, outs, args, 1800000000, 20000000, far=(9,), scratch=WEIGHTS, name="between")


BACK = WEIGHTS + (
    pltpu.VMEM((ROWS, D), bf16),
    pltpu.VMEM((ROWS, 3 * D), bf16),
    pltpu.VMEM((ROWS, D), bf16),
)


def second_back(
    place,
    back,
    slot_column,
    cotangent,
    middle,
    shares,
    own,
    flipped,
    feed,
    joint,
    stream,
    weights,
    first_shares,
    slot_row,
):
    def body(
        place,
        back,
        slot_column,
        cotangent,
        middle,
        shares,
        own,
        flipped,
        feed,
        joint,
        stream,
        far,
        first_shares,
        slot_row,
        low_out,
        grad_out,
        mine,
        other,
        small_out,
        grad_dense,
        send,
        near,
        sems,
        mixed,
        joint_grad,
        attended,
    ):
        copies = start_weights(far, near, sems)
        expert, from_experts = take_second(back, slot_column)
        total = own[...] + flipped[...].astype(f32)
        dense, from_feed = total[:, 0:D], total[:, D : 2 * D]
        one, two = shares[:, 0:1], shares[:, 1:2]
        low_out[...] = (middle[...] + one * dense + two * expert).astype(bf16)
        gradient = backward(
            stream[...],
            near,
            copies,
            joint,
            middle[...],
            feed[:, 0:D],
            one,
            two,
            cotangent[...].astype(f32),
            dense,
            expert,
            from_feed + from_experts,
            joint_grad,
            attended,
            small_out,
            mixed,
        )
        grad_out[...] = gradient
        grad_dense[...] = (gradient * first_shares[:, 0:1]).astype(bf16)
        send_first((gradient * first_shares[:, 1:2]).astype(bf16), slot_row, send)
        for out, core in ((mine, place[1]), (other, 1 - place[1])):
            wide = pl.multiple_of(core * 1536, 128)
            out[:, 0:1536] = joint_grad[:, pl.ds(wide, 1536)]
            out[:, 1536:2048] = attended[:, pl.ds(pl.multiple_of(core * 512, 128), 512)]

    outs = (
        shape(ROWS, D),
        shape(ROWS, D, dtype=f32),
        shape(ROWS, 2048),
        shape(ROWS, 2048),
        shape(8, D, dtype=f32),
        shape(ROWS, D),
        shape(1024, D),
    )
    args = (
        place,
        back,
        slot_column,
        cotangent,
        middle,
        shares,
        own,
        flipped,
        feed,
        joint,
        stream,
        weights,
        first_shares,
        slot_row,
    )
    return call(body, outs, args, 1000000, 1000000, far=(11,), scratch=BACK, name="turn")


def first_back(
    place, back, slot_column, upstream, middle, shares, dense, expert, own, parts, normed_two, joint, tokens, weights
):
    def body(
        place,
        back,
        slot_column,
        upstream,
        middle,
        shares,
        dense,
        expert,
        own,
        part_a,
        part_b,
        part_c,
        normed_two,
        joint,
        tokens,
        far,
        grad_out,
        mine,
        other,
        small_out,
        near,
        sems,
        mixed,
        joint_grad,
        attended,
    ):
        copies = start_weights(far, near, sems)
        incoming = take_first(back, slot_column)
        incoming = (
            own[...]
            + part_a[...].astype(f32)
            + part_b[...].astype(f32)
            + part_c[...].astype(f32)
            + incoming
        )
        grad_out[...] = backward(
            tokens[...].astype(f32),
            near,
            copies,
            joint,
            middle[...],
            normed_two[...],
            shares[:, 0:1],
            shares[:, 1:2],
            upstream[...],
            dense[...],
            expert[...],
            incoming,
            joint_grad,
            attended,
            small_out,
            mixed,
        )
        for out, core in ((mine, place[1]), (other, 1 - place[1])):
            for i, step in enumerate((0, 1, 3, 2)):
                index = lax.rem(place[0] + step, 4) * 2 + core
                wide = pl.ds(pl.multiple_of(index * 384, 128), 384)
                out[i, :, 0:384] = joint_grad[:, wide]
                out[i, :, 384:512] = attended[:, pl.ds(pl.multiple_of(index * 128, 128), 128)]

    outs = (
        shape(ROWS, D, dtype=f32),
        shape(4, ROWS, 512),
        shape(4, ROWS, 512),
        shape(8, D, dtype=f32),
    )
    args = (
        place,
        back,
        slot_column,
        upstream,
        middle,
        shares,
        dense,
        expert,
        own,
        *parts,
        normed_two,
        joint,
        tokens,
        weights,
    )
    return call(body, outs, args, 1000000, 1000000, far=(15,), scratch=BACK, name="back")


def few_columns(small):
    pick = lax.broadcasted_iota(jnp.int32, (8, 128), 0) == lax.broadcasted_iota(
        jnp.int32, (8, 128), 1
    )
    return dot_tn(small[...].astype(bf16), pick.astype(bf16)).astype(bf16)


def weights_first(place, line, mine, got, parts, small):
    def body(place, line, mine, got, part_a, part_b, part_c, small, out, ordered):
        def put(step, core, value):
            index = lax.rem(place[0] + step, 4) * 2 + core
            ordered[pl.ds(pl.multiple_of(index * ROWS, ROWS), ROWS), :] = value

        own, other = place[1], 1 - place[1]
        put(0, own, mine[0])
        put(0, other, got[0])
        for step, part in ((3, part_a), (1, part_b), (2, part_c)):
            put(step, own, part[0:ROWS, :])
            put(step, other, part[ROWS : 2 * ROWS, :])
        for low in range(0, D, 256):
            rows = slice(low, low + 256)
            for left, first, last in ((low, 0, 384), (D + low, 384, 512)):
                out[rows, first:last] = dot_tn(
                    line[:, left : left + 256], ordered[:, first:last]
                ).astype(bf16)
        out[:, 512:640] = few_columns(small)

    args = (place, line, mine, got, *parts, small)
    return call(
        body,
        (shape(D, 640),),
        args,
        1000000,
        1000000,
        scratch=(pltpu.VMEM((1024, 512), bf16),),
        name="first_weights",
    )[0]


def weights_second(packed, pair, pair_twin, mine, got, small):
    def body(packed, pair, pair_twin, mine, got, small, out, near, sem):
        for low in range(0, D, 256):
            rows = slice(low, low + 256)
            for left, first, last in ((low, 0, 1536), (D + low, 1536, 2048)):
                near[rows, first:last] = (
                    dot_tn(pair[:, left : left + 256], mine[:, first:last])
                    + dot_tn(pair_twin[:, left : left + 256], got[:, first:last])
                ).astype(bf16)
        near[:, 2048:2176] = few_columns(small)
        copy = pltpu.make_async_copy(near, out.at[:, 2048:4224], sem)
        copy.start()
        copy.wait()

    args = (packed, pair, pair_twin, mine, got, small)
    return pl.pallas_call(
        body,
        out_shape=shape(D, 4224),
        in_specs=[pl.BlockSpec(memory_space=pl.ANY)] + [whole()] * 5,
        out_specs=pl.BlockSpec(memory_space=pl.ANY),
        scratch_shapes=[pltpu.VMEM((D, 2176), bf16), pltpu.SemaphoreType.DMA(())],
        input_output_aliases={0: 0},
        compiler_params=pltpu.CompilerParams(vmem_limit_bytes=LIMIT),
        cost_estimate=pl.CostEstimate(flops=1000000, bytes_accessed=1000000, transcendentals=0),
        name="second_weights",
    )(*args)


def weights_feed(place, group, group_twin, grad_hidden, active, got, inc, inc_twin):
    def body(place, group, group_twin, grad_hidden, active, got, inc, inc_twin, out):
        base = place[1] * 512
        grad = grad_hidden[:, pl.ds(pl.multiple_of(base, 128), 512)]
        for low in range(0, D, 256):
            rows = slice(low, low + 256)
            out[rows, 0:512] = (
                dot_tn(group[:, rows], grad) + dot_tn(group_twin[:, rows], got[:, 0:512])
            ).astype(bf16)
        for low in range(0, 512, 256):
            units = active[:, pl.ds(pl.multiple_of(base + low, 128), 256)]
            narrow = (
                dot_tn(units, inc[...]) + dot_tn(got[:, 512 + low : 768 + low], inc_twin[...])
            ).astype(bf16)
            for i in range(8):
                start = low * 2 + i * 64
                part = narrow[i * 32 : (i + 1) * 32, :]
                out[start : start + 32, 512:1024] = part[:, 0:512]
                out[start + 32 : start + 64, 512:1024] = part[:, 512:1024]

    args = (place, group, group_twin, grad_hidden, active, got, inc, inc_twin)
    return call(body, (shape(D, 1024),), args, 1000000, 1000000, name="feed_weights")[0]


def feed_forward(group, packed):
    def body(group, far, own, part_a, part_b, part_c, active_out, slope_out, narrow, near, sem):
        copy = pltpu.make_async_copy(far.at[:, PACKED : PACKED + 2 * D], near, sem)
        copy.start()
        copy.wait()
        for i in range(16):
            for core in range(2):
                source = (i * 2 + core) * 32
                target = core * 512 + i * 32
                narrow[target : target + 32, :] = near[source : source + 32, D : 2 * D]
        for low in range(0, 512, 256):
            place = slice(low, low + 256)
            active, slope = gelu_pieces(dot(group[place, :], near[:, 0:D]))
            active = active.astype(bf16)
            active_out[place, :] = active
            slope_out[place, :] = slope.astype(bf16)
            terms = dot(active, narrow[...])
            first, second = ((own, part_a), (part_b, part_c))[low // 256]
            first[...] = terms[0:ROWS].astype(first.dtype)
            second[...] = terms[ROWS : 2 * ROWS].astype(bf16)

    outs = (
        shape(ROWS, D, dtype=f32),
        shape(ROWS, D),
        shape(ROWS, D),
        shape(ROWS, D),
        shape(512, D),
        shape(512, D),
        shape(D, D),
    )
    scratch = (pltpu.VMEM((D, 2 * D), bf16), pltpu.SemaphoreType.DMA(()))
    args = (group, packed)
    own, *parts, active, slope, narrow = call(
        body, outs, args, 1000000, 1000000, far=(1,), scratch=scratch, name="feed_one"
    )
    return own, return_parts(parts), active, slope, narrow


def feed_backward(place, group, active, slope, narrow, packed):
    def body(
        place, group, active, slope, narrow, far, own, part_a, part_b, part_c, grad_out, sent, near, sem
    ):
        copy = pltpu.make_async_copy(far.at[:, PACKED : PACKED + D], near, sem)
        copy.start()
        other = pl.ds(pl.multiple_of((1 - place[1]) * 512, 128), 512)
        sent[:, 512:1024] = active[:, other]
        for low in range(0, 512, 256):
            rows = slice(low, low + 256)
            grad = dot_nt(group[rows, :], narrow[...]) * slope[rows, :].astype(f32)
            grad = grad.astype(bf16)
            grad_out[rows, :] = grad
            if low == 0:
                copy.wait()
            terms = dot_nt(grad, near[...])
            first, second = ((own, part_a), (part_b, part_c))[low // 256]
            first[...] = terms[0:ROWS].astype(first.dtype)
            second[...] = terms[ROWS : 2 * ROWS].astype(bf16)
        sent[:, 0:512] = grad_out[:, other]

    outs = (
        shape(ROWS, D, dtype=f32),
        shape(ROWS, D),
        shape(ROWS, D),
        shape(ROWS, D),
        shape(512, D),
        shape(512, D),
    )
    scratch = (pltpu.VMEM((D, D), bf16), pltpu.SemaphoreType.DMA(()))
    args = (place, group, active, slope, narrow, packed)
    own, *parts, grad, sent = call(
        body, outs, args, 1000000, 1000000, far=(5,), scratch=scratch, name="feed_one_back"
    )
    return own, return_parts(parts), grad, sent


def gelu_pieces(x):
    k = 0.7978845608028654
    square = x * x
    bend = jnp.tanh(k * (x + 0.044715 * (square * x)))
    half = 0.5 * (1.0 + bend)
    slope = half + x * (0.5 * (1.0 - bend * bend)) * (k * (1.0 + 3 * 0.044715 * square))
    return x * half, slope


def grid_call(body, grid, in_specs, outs, out_specs, scratch, args, flops, moved, name):
    return pl.pallas_call(
        body,
        grid=grid,
        in_specs=in_specs,
        out_shape=outs,
        out_specs=out_specs,
        scratch_shapes=scratch,
        compiler_params=pltpu.CompilerParams(
            vmem_limit_bytes=LIMIT, dimension_semantics=("arbitrary",)
        ),
        cost_estimate=pl.CostEstimate(flops=flops, bytes_accessed=moved, transcendentals=0),
        name=name,
    )(*args)


def fixed(rows, columns):
    return pl.BlockSpec(
        (rows, columns), lambda i: (0, 0), pipeline_mode=pl.Buffered(buffer_count=1)
    )


def rows_of(rows, columns):
    return pl.BlockSpec((rows, columns), lambda i: (i, 0))


def owner_forward(rows, expander, reducer):
    def body(rows, expander, reducer, active_out, slope_out, parts_out):
        active, slope = gelu_pieces(dot(rows[...], expander[...]))
        active = active.astype(bf16)
        active_out[...] = active
        slope_out[...] = slope.astype(bf16)
        parts_out[...] = dot(active, reducer[...]).astype(bf16)

    block = rows_of(512, D)
    return grid_call(
        body,
        (2,),
        [block, fixed(D, D), fixed(D, D)],
        (shape(1024, D),) * 3,
        [block] * 3,
        [],
        (rows, expander, reducer),
        4300000000,
        12000000,
        "owner",
    )


def owner_backward(incoming, slope, expander, reducer):
    def body(incoming, slope, expander, reducer, grad_out, rows_out):
        grad = (dot_nt(incoming[...], reducer[...]) * slope[...].astype(f32)).astype(bf16)
        grad_out[...] = grad
        rows_out[...] = dot_nt(grad, expander[...]).astype(bf16)

    block = rows_of(256, D)
    return grid_call(
        body,
        (4,),
        [block, block, fixed(D, D), fixed(D, D)],
        (shape(1024, D),) * 2,
        [block] * 2,
        [],
        (incoming, slope, expander, reducer),
        4300000000,
        12000000,
        "owner_back",
    )


def places(kind):
    row = lax.broadcasted_iota(jnp.int32, (128, 256), 0)
    column = lax.broadcasted_iota(jnp.int32, (128, 256), 1)
    return (column == (row // 4) * 8 + kind * 4 + row % 4).astype(bf16)


def owner_both(arrived, expander, reducer):
    def body(arrived, expander, reducer, rows, grads, active_out, grad_out, sent):
        for block in range(2):
            packed = arrived[block * 256 : (block + 1) * 256, :]
            place = slice(block * 128, (block + 1) * 128)
            rows[place, :] = dot(places(0), packed).astype(bf16)
            grads[place, :] = dot(places(1), packed).astype(bf16)
        for low in range(0, 2048, 512):
            units = slice(low, low + 512)
            active, slope = gelu_pieces(dot(rows[...], expander[:, units]))
            active_out[:, units] = active.astype(bf16)
            grad_out[:, units] = (dot_nt(grads[...], reducer[units, :]) * slope).astype(bf16)
        parts = dot(active_out[...], reducer[...]).astype(bf16)
        returned = dot_nt(grad_out[...], expander[...]).astype(bf16)
        for block in range(2):
            place = slice(block * 128, (block + 1) * 128)
            sent[block * 256 : (block + 1) * 256, :] = (
                dot_tn(places(0), parts[place]) + dot_tn(places(1), returned[place])
            ).astype(bf16)

    return grid_call(
        body,
        (2,),
        [rows_of(512, D), fixed(D, 2048), fixed(2048, D)],
        (shape(512, D), shape(512, D), shape(512, 2048), shape(512, 2048), shape(1024, D)),
        [rows_of(256, D), rows_of(256, D), rows_of(256, 2048), rows_of(256, 2048), rows_of(512, D)],
        [],
        (arrived, expander, reducer),
        9000000000,
        20000000,
        "owner_both",
    )


def feed_both(place, mine, partner, weights):
    def body(place, mine, partner, far, own, other, active, grad, sent, rows, near, sems):
        copies = []
        for i, low in enumerate((0, 2 * D, D, 3 * D)):
            copy = pltpu.make_async_copy(
                far.at[:, low : low + D], near.at[:, low : low + D], sems.at[i]
            )
            copy.start()
            copies.append(copy)
        rows[0:ROWS, :] = mine[...]
        rows[ROWS : 2 * ROWS, :] = partner[...]
        for part in range(2):
            units = slice(part * D, part * D + D)
            narrow = slice(2 * D + part * D, 3 * D + part * D)
            copies[2 * part].wait()
            value, slope = gelu_pieces(dot(rows[:, 0:D], near[:, units]))
            active[:, units] = value.astype(bf16)
            copies[2 * part + 1].wait()
            back = dot_nt(rows[:, D : 2 * D], near[:, narrow]) * slope
            grad[:, units] = back.astype(bf16)
        dense = dot(active[:, 0:D], near[:, 2 * D : 3 * D]) + dot(
            active[:, D : 2 * D], near[:, 3 * D : 4 * D]
        )
        own[:, 0:D] = dense[0:ROWS]
        other[:, 0:D] = dense[ROWS : 2 * ROWS].astype(bf16)
        back = dot_nt(grad[...], near[:, 0 : 2 * D])
        own[:, D : 2 * D] = back[0:ROWS]
        other[:, D : 2 * D] = back[ROWS : 2 * ROWS].astype(bf16)
        twin = pl.ds(pl.multiple_of((1 - place[1]) * D, 128), D)
        sent[:, 0:D] = active[:, twin]
        sent[:, D : 2 * D] = grad[:, twin]

    outs = (
        shape(ROWS, 2 * D, dtype=f32),
        shape(ROWS, 2 * D),
        shape(2 * ROWS, 2 * D),
        shape(2 * ROWS, 2 * D),
        shape(2 * ROWS, 2 * D),
    )
    scratch = (
        pltpu.VMEM((2 * ROWS, 2 * D), bf16),
        pltpu.VMEM((D, 4 * D), bf16),
        pltpu.SemaphoreType.DMA((4,)),
    )
    args = (place, mine, partner, weights)
    return call(body, outs, args, 1000000, 1000000, far=(3,), scratch=scratch, name="feed")


def feed_gradients(place, mine, partner, twins, active, grad, got):
    def body(place, mine, partner, twins, active, grad, got, out):
        base = place[1] * D

        for low in range(0, D, 256):
            column = slice(low, low + 256)
            units = pl.ds(pl.multiple_of(base + low, 128), 256)
            normed = slice(low, low + 256)
            values = grad[:, pl.ds(pl.multiple_of(base, 128), D)]
            out[column, 0:D] = (
                dot_tn(mine[:, normed], values[0:ROWS])
                + dot_tn(partner[:, normed], values[ROWS : 2 * ROWS])
                + dot_tn(twins[:, normed], got[:, D : 2 * D])
            ).astype(bf16)
            out[column, D : 2 * D] = (
                dot_tn(active[0:ROWS, units], mine[:, D : 2 * D])
                + dot_tn(active[ROWS : 2 * ROWS, units], partner[:, D : 2 * D])
                + dot_tn(got[:, column], twins[:, D : 2 * D])
            ).astype(bf16)

    args = (place, mine, partner, twins, active, grad, got)
    outs = (shape(D, 4224),)
    return pl.pallas_call(
        body,
        grid=(1,),
        in_specs=[pl.BlockSpec(memory_space=pltpu.SMEM)]
        + [pl.BlockSpec(arg.shape, lambda i: (0, 0)) for arg in args[1:]],
        out_shape=outs,
        out_specs=[pl.BlockSpec((D, 2 * D), lambda i: (0, 0))],
        compiler_params=pltpu.CompilerParams(vmem_limit_bytes=LIMIT),
        cost_estimate=pl.CostEstimate(flops=1000000, bytes_accessed=1000000, transcendentals=0),
        name="feed_gradients",
    )(*args)[0]


def after(value, *others):
    return lax.optimization_barrier((value, *others))[0]


def gather_line(value):
    return jnp.concatenate(around(value), axis=0)


def return_parts(parts):
    return shift(parts[0], "z", -1), shift(parts[1], "z", 1), shift(parts[2], "z", 2)


def around(value):
    return value, shift(value, "z", 1), shift(value, "z", -1), shift(value, "z", 2)


def positions(route):
    chosen = route[:, 0]
    row = jnp.arange(ROWS, dtype=jnp.int32)
    earlier = (row[None, :] < row[:, None]) & (row[None, :] // SEQ == row[:, None] // SEQ)
    same = (chosen[None, :] == chosen[:, None]) & earlier
    return chosen, row // SEQ, jnp.sum(same.astype(jnp.int32), axis=1)


def slots_first(route):
    chosen, sequence, position = positions(route)
    slot = chosen * 8 + sequence * 4 + position
    return slot[:, None], slot[None, :]


def slots_second(route):
    chosen, sequence, position = positions(route)
    slot = (chosen // 32) * 256 + (chosen % 32) * 8 + sequence * 2 + position
    return slot[:, None], slot[None, :]


def exchange(rows):
    blocks = rows.reshape(128, 8, rows.shape[-1])
    moved = lax.all_to_all(blocks, ALL, split_axis=0, concat_axis=0, tiled=True)
    return moved.reshape(rows.shape)


def exchange_plane(packed):
    blocks = packed.reshape(16, 64, packed.shape[1])
    return lax.all_to_all(blocks, PLANE, split_axis=0, concat_axis=0, tiled=True)


def few_rows(few):
    pick = lax.broadcasted_iota(jnp.int32, (8, 128), 0) == lax.broadcasted_iota(
        jnp.int32, (8, 128), 1
    )
    return lax.dot_general(
        pick.astype(f32),
        few,
        (((1,), (1,)), ((), ())),
        precision=lax.Precision.HIGHEST,
        preferred_element_type=f32,
    )


def write_few(total, mixer, gain, regain):
    rows = few_rows(total)
    mixer[...] = rows[0:2]
    gain[...] = rows[2:3]
    regain[...] = rows[3:4]


FEW = (
    jax.ShapeDtypeStruct((2, 32), f32),
    jax.ShapeDtypeStruct((1, 32), f32),
    jax.ShapeDtypeStruct((1, 32), f32),
)


def add_blocks(blocks):
    return jnp.sum(blocks.astype(f32), axis=0).astype(bf16)


def pack_attention(inner, outer, mixer, gain, regain):
    blank = jnp.zeros((inner.shape[0], 124), bf16)
    return jnp.concatenate([inner, outer, mixer, gain[:, None], regain[:, None], blank], axis=1)


def pack_feed_first(widen, narrow):
    z = lax.axis_index("z")
    units = widen.reshape(32, 16, 2, 4, 32)
    units = lax.dynamic_index_in_dim(units, z, 3, keepdims=False)
    columns = units.transpose(0, 2, 1, 3).reshape(32, 1024)
    return jnp.concatenate([columns, lax.dynamic_slice_in_dim(narrow, z * 32, 32, 0)], axis=1)


def pack_feed_second(widen, narrow):
    half = lax.rem(lax.axis_index("z"), 2)
    units = widen.reshape(32, 16, 2, 2, 2, 32)
    units = lax.dynamic_index_in_dim(units, half, 3, keepdims=False)
    columns = units.transpose(0, 3, 1, 2, 4).reshape(32, 2048)
    rows = half_of(narrow, half, 0)
    return jnp.concatenate([columns, rows[:32], rows[32:]], axis=1)


def quarter(place, i):
    return lax.rem(place[0] + (0, 3, 1, 2)[i], 4)


def finish_second(place, summed):
    c = lax.axis_index("c")
    got = swap(lax.dynamic_slice_in_dim(summed, 32 * (1 - c), 32, 1))

    def body(place, summed, got, widen, narrow, inner, outer, mixer, gain, regain):
        lane = lax.broadcasted_iota(jnp.int32, (32, 128), 1) // 32
        rows = pl.ds(pl.multiple_of(place[1] * 32, 32), 32)

        def mine(z, low, size):
            return summed[z, rows, low : low + size].astype(f32)

        def twin(z, low, size):
            return got[z, :, low : low + size].astype(f32)

        for index, (core, term) in enumerate(((place[1], mine), (1 - place[1], twin))):
            for low in range(0, 1024, 128):
                for half in range(2):
                    value = term(half, low, 128) + term(half + 2, low, 128)
                    target = half * 2 + core
                    for k in range(4):
                        moved = pltpu.roll(value, lax.rem(target * 32 + (128 - k * 32), 128), 1)
                        column = (low // 32 + k) * 128
                        out = widen.at[:, column : column + 128]
                        if index == 0 and half == 0:
                            out[...] = moved
                        else:
                            out[...] = jnp.where(lane == target, moved, out[...])
            for half in range(2):
                place_in = pl.multiple_of(half * 64 + core * 32, 32)
                narrow[pl.ds(place_in, 32), :] = term(half, 1024, 1024) + term(half + 2, 1024, 1024)
            for out, low, size in ((inner, 2048, 1536), (outer, 3584, 512)):
                total = (term(0, low, size) + term(1, low, size)) + (
                    term(2, low, size) + term(3, low, size)
                )
                out[:, pl.ds(pl.multiple_of(core * size, 128), size)] = total
        total = jnp.zeros((32, 128), f32)
        for z in range(4):
            total += mine(z, 4096, 128) + twin(z, 4096, 128)
        write_few(total, mixer, gain, regain)

    outs = (
        shape(32, 4096, dtype=f32),
        shape(ROWS, D, dtype=f32),
        shape(32, 3072, dtype=f32),
        shape(32, D, dtype=f32),
        *FEW,
    )
    widen, narrow, inner, outer, mixer, gain, regain = call(
        body, outs, (place, summed, got), 1000000, 1000000, name="second_out"
    )
    return (widen, narrow), (inner, outer), (mixer.T, gain.reshape(32), regain.reshape(32))


def finish_feed_first(place, blocks):
    c = lax.axis_index("c")
    summed = add_blocks(blocks)
    widen = summed[:, :512]
    widen = in_order(c, half_of(widen, c, 0), swap(half_of(widen, 1 - c, 0)), 1)
    narrow = jnp.concatenate([summed[:32, 512:], summed[32:, 512:]], axis=1)
    pieces = around(jnp.concatenate([widen, narrow], axis=0))

    def body(place, own, before, later, opposite, widen, narrow):
        lane = lax.broadcasted_iota(jnp.int32, (32, 128), 1) // 32
        for i, source in enumerate((own, before, later, opposite)):
            z = quarter(place, i)
            narrow[pl.ds(pl.multiple_of(z * 32, 32), 32), :] = source[32:64, :].astype(f32)
            for core in range(2):
                for four in range(4):
                    column = core * 512 + four * 128
                    value = source[0:32, column : column + 128].astype(f32)
                    for k in range(4):
                        moved = pltpu.roll(value, lax.rem(z * 32 + (128 - k * 32), 128), 1)
                        low = (four * 4 + k) * 256 + core * 128
                        out = widen.at[:, low : low + 128]
                        if i == 0:
                            out[...] = moved
                        else:
                            out[...] = jnp.where(lane == z, moved, out[...])

    outs = (shape(32, 4096, dtype=f32), shape(ROWS, D, dtype=f32))
    return call(body, outs, (place, *pieces), 1000000, 1000000, name="feed_one_out")


def finish_attention_first(place, blocks, earlier):
    summed = jnp.sum(blocks.reshape(16, 2, 32, 640).astype(f32), axis=0).astype(bf16)
    pieces = lax.optimization_barrier((*around(summed), earlier))[:4]

    def body(place, own, before, later, opposite, inner, outer, mixer, gain, regain):
        sources = (own, before, later, opposite)
        halves = []
        for core in range(2):
            one, two, three, four = (x[core, :, 512:640].astype(f32) for x in sources)
            halves.append((one + four) + (two + three))
        write_few(halves[0] + halves[1], mixer, gain, regain)
        for i, source in enumerate(sources):
            z = quarter(place, i)
            for core in range(2):
                index = z * 2 + core
                inner[:, pl.ds(pl.multiple_of(index * 384, 128), 384)] = source[
                    core, :, 0:384
                ].astype(f32)
                outer[:, pl.ds(pl.multiple_of(index * 128, 128), 128)] = source[
                    core, :, 384:512
                ].astype(f32)

    outs = (shape(32, 3072, dtype=f32), shape(32, D, dtype=f32), *FEW)
    inner, outer, mixer, gain, regain = call(
        body, outs, (place, *pieces), 1000000, 1000000, name="attention_out"
    )
    return inner, outer, mixer.T, gain.reshape(32), regain.reshape(32)


def on_device(
    tokens,
    cotangent,
    routes_first,
    routes_second,
    inner_first,
    outer_first,
    widen_first,
    narrow_first,
    mixer_first,
    gain_first,
    regain_first,
    inner_second,
    outer_second,
    widen_second,
    narrow_second,
    mixer_second,
    gain_second,
    regain_second,
    expand_first,
    reduce_first,
    expand_second,
    reduce_second,
):
    place = jnp.stack([lax.axis_index("z"), lax.axis_index("c")]).astype(jnp.int32)
    gathered_first = lax.all_gather(
        jnp.concatenate(
            [
                pack_attention(inner_first, outer_first, mixer_first, gain_first, regain_first),
                pack_feed_first(widen_first, narrow_first),
            ],
            axis=1,
        ),
        ("x", "y", "c"),
        axis=0,
        tiled=True,
    )
    gathered_second = lax.all_gather(
        pack_attention(inner_second, outer_second, mixer_second, gain_second, regain_second),
        ("x", "y", "c"),
        axis=0,
        tiled=True,
    )
    gathered_feed = lax.all_gather(
        pack_feed_second(widen_second, narrow_second), ("x", "y", "c"), axis=0, tiled=True
    )
    column_first, row_first = slots_first(routes_first)
    column_second, row_second = slots_second(routes_second)
    expander, reducer = expand_first[0], reduce_first[0]

    pair, joint, middle, normed_two, shares, send = first_front(tokens, gathered_first, row_first)
    received = exchange(send)
    group = gather_line(normed_two)
    received = after(received, group)
    active, slope, parts = owner_forward(received, expander, reducer)
    back = exchange(parts)
    dense_own, dense_parts, active_feed, slope_feed, narrow_one = feed_forward(
        after(group, parts), gathered_first
    )

    output, stream, dense, expert, pair_s, joint_s, middle_s, feed_s, shares_s, send = second_front(
        back,
        column_first,
        middle,
        shares,
        dense_own,
        dense_parts,
        cotangent,
        gathered_second,
        row_second,
    )
    arrived = exchange(send)
    feed_flipped = flip(feed_s)
    arrived = after(arrived, feed_flipped)
    line = lax.all_gather(after(pair, arrived), COLUMN, axis=0, tiled=True)
    rows, incoming_s, active_s, grad_s, sent = owner_both(
        arrived, expand_second[0], reduce_second[0]
    )
    back = exchange(sent)
    terms, terms_partner, active_second, grad_second, feed_sent = feed_both(
        place, feed_s, after(feed_flipped, sent), gathered_feed
    )
    flipped = flip(terms_partner)
    feed_gradient = feed_gradients(
        place,
        feed_s,
        feed_flipped,
        swap(jnp.concatenate([feed_s, feed_flipped], axis=0)),
        active_second,
        grad_second,
        swap(feed_sent),
    )
    back = after(back, feed_gradient)
    pair_twin = swap(pair_s)
    back = after(back, line, pair_twin)
    output_two, upstream, mine, other, small, grad_dense, send = second_back(
        place,
        back,
        column_second,
        cotangent,
        middle_s,
        shares_s,
        terms,
        flipped,
        feed_s,
        joint_s,
        stream,
        gathered_second,
        shares,
        row_first,
    )
    grad_s = after(grad_s, send)
    grad_expand_two = dot_tn(rows, grad_s)
    grad_reduce_two = dot_tn(active_s, after(incoming_s, send))

    grad_group = gather_line(grad_dense)
    incoming = after(exchange(send), grad_expand_two, grad_reduce_two, grad_group)
    grad_first, grad_rows = owner_backward(incoming, slope, expander, reducer)
    feed_own, feed_parts, grad_hidden, feed_sent = feed_backward(
        place,
        after(grad_group, grad_rows),
        active_feed,
        slope_feed,
        narrow_one,
        gathered_first,
    )
    packed = weights_second(feed_gradient, pair_s, pair_twin, mine, swap(other), small)
    packed = lax.psum_scatter(packed, PLANE, scatter_dimension=0, tiled=True)
    back = exchange(grad_rows)
    feed_packed = weights_feed(
        place,
        group,
        swap(group),
        grad_hidden,
        active_feed,
        swap(feed_sent),
        grad_group,
        swap(grad_group),
    )
    grad_expand_one = dot_tn(received, grad_first)
    grad_reduce_one = dot_tn(active, incoming)
    back = after(back, grad_expand_one, grad_reduce_one, *feed_parts)
    back = after(back, feed_packed)
    feed_sums = exchange_plane(after(feed_packed, back))
    gradient_tokens, mine, other, small = first_back(
        place,
        back,
        column_first,
        upstream,
        middle,
        shares,
        dense,
        expert,
        feed_own,
        feed_parts,
        normed_two,
        joint,
        tokens,
        gathered_first,
    )
    got = swap(other)
    ahead = [jnp.concatenate([mine[i], got[i]], axis=0) for i in (1, 2, 3)]
    parts = (shift(ahead[0], "z", 1), shift(ahead[1], "z", -1), shift(ahead[2], "z", 2))
    first_packed = weights_first(place, line, mine, got, parts, small)
    first_packed = after(first_packed, feed_sums)
    packed = lax.all_gather(after(packed, first_packed), "z", axis=0)
    blocks = lax.all_to_all(
        first_packed.reshape(32, 32, 640), ("x", "y", "c"), split_axis=0, concat_axis=0, tiled=True
    )
    feed_finals = finish_feed_first(place, feed_sums)
    packed = after(packed, feed_finals)
    feed_finals_second, finals_second, few_second = finish_second(place, packed)
    inner, outer, *few_first = finish_attention_first(
        place, blocks, (feed_finals, feed_finals_second, finals_second)
    )
    return (
        (output, output_two, gradient_tokens)
        + (inner, outer)
        + tuple(feed_finals)
        + tuple(few_first)
        + finals_second
        + tuple(feed_finals_second)
        + few_second
        + (
            grad_expand_one[None],
            grad_reduce_one[None],
            grad_expand_two[None],
            grad_reduce_two[None],
        )
    )


def solution(mesh):
    fine = Mesh(mesh.devices.reshape(4, 4, 4, 2), ALL)
    owner = ("x", "y", "c")
    tokens = P(ALL, None)
    dense = (P(owner, None),) * 5 + (P(owner),) * 2
    experts = (
        P(owner, None, "z"),
        P(owner, "z", None),
        P(ALL, None, None),
        P(ALL, None, None),
    )
    return jax.shard_map(
        on_device,
        mesh=fine,
        in_specs=(tokens,) * 4 + dense + dense + experts,
        out_specs=(tokens,) * 3 + dense + dense + experts,
        check_vma=False,
    )
```
